512 devices in a mesh: dp: 4 (over x), ctx: 16 (over z_hi, y), head: 8 (over z_lo, core).
Axes of the slice: x: 4, y: 8, z: 8 (z_hi: 2, z_lo: 4; z = z_hi * 4 + z_lo), core: 2. Of those that a mesh axis runs over, the one named last changes fastest.
Arguments:
- queries: bfloat16 [4, 2560, 8192], P('dp', 'ctx', 'head'), may hold values from -6 to 6
- keys_values: bfloat16 [2, 4, 2560, 1024], P(None, 'dp', 'ctx', 'head'), may hold values from -6 to 6
- out_grad: bfloat16 [4, 2560, 8192], P('dp', 'ctx', 'head'), may hold values from -6 to 6
- activations: bfloat16 [4, 2560, 8192], P('dp', 'ctx', 'head'), may hold values from -6 to 6
- adapter_down: bfloat16 [3, 16, 8192], P(None, None, 'head'), may hold values from -0.0625 to 0.0625
- adapter_up_q: bfloat16 [16, 8192], P(None, 'head'), may hold values from -0.0625 to 0.0625
- adapter_up_kv: bfloat16 [2, 16, 1024], P(None, None, 'head'), may hold values from -0.1875 to 0.1875
- doc_lengths: int32 [4, 8], P('dp'), may hold values from 1 to 1280, 2560 in all within a row
- block_order: int32 [32], replicated, may hold values from 0 to 31, each once
Outputs:
- grad_queries: bfloat16 [4, 2560, 8192], P('dp', 'ctx', 'head')
- grad_keys_values: bfloat16 [2, 4, 2560, 1024], P(None, 'dp', 'ctx', 'head')
- grad_down: float32 [3, 16, 8192], P(None, None, 'head')
- grad_up_q: float32 [16, 8192], P(None, 'head')
- grad_up_kv: float32 [2, 16, 1024], P(None, None, 'head')
The draws below stay inside these ranges and needn't reach their ends.
Inputs may be any that keep to these rules, and one draw needn't show every extreme that they name: `doc_lengths`: each row sums to 2560; its largest entry is exactly 1280. `block_order`: each of 0 .. 31 once.
All inputs are finite; a program needn't handle non-finite values.
Results may differ from the reference program's by a relative error of at most 0.017.
Values may be sent and summed in bfloat16 or wider, within the bound.
A program may use at most 64 MiB of HBM per device.

```python
import math
import jax
import jax.numpy as jnp
import numpy as np
from jax import lax

D = 8192
HD = 128
GROUP = 8
RANK = 16
DOCS = 8
ROWS_DEV = 160
KV_HEADS = 8
Q_HEADS = 64
BLOCK = 80
SLOTS = 32
SEQ = 2560
BATCH = 4
DOC_MOST = 1280
N_CTX = 16


def draw_queries(key, part):
    key = jax.random.fold_in(key, 11)
    extent = (BATCH, SEQ, Q_HEADS * HD)
    values_drawn = jax.random.truncated_normal(key, -6.0, 6.0, extent, jnp.float32)
    return values_drawn.astype(jnp.bfloat16)


def draw_keys_values(key, part):
    key = jax.random.fold_in(key, 23)
    extent = (2, BATCH, SEQ, KV_HEADS * HD)
    values_drawn = jax.random.truncated_normal(key, -6.0, 6.0, extent, jnp.float32)
    return values_drawn.astype(jnp.bfloat16)


def shard_levels(rng, dims, cuts, least, high):
    def one(axis_at, shards_of):
        heights = jax.random.uniform(jax.random.fold_in(jax.random.fold_in(rng, 6), axis_at), (shards_of,), jnp.float32, least / len(cuts), high / len(cuts))
        return jnp.repeat(jnp.exp(heights), dims[axis_at] // shards_of).reshape((-1,) + (1,) * (len(dims) - axis_at - 1))

    factor_of = one(*cuts[0])
    for cut in cuts[1:]:
        factor_of = factor_of * one(*cut)
    return factor_of


def profile(amount, total, reach, slope):
    loads = [(1 << 20) // math.isqrt(grade ** slope) + 1 for grade in range(2, amount + 1)]
    surplus, counts = total - reach - (amount - 1), [1] * (amount - 1)
    while surplus > 0:
        candidates = [i for i in range(amount - 1) if counts[i] < reach]
        pool, left = sum([loads[i] for i in candidates]), surplus
        for i in candidates:
            more = min(reach - counts[i], max(1, left * loads[i] // pool), surplus)
            counts[i] = counts[i] + more
            surplus = surplus - more
    return np.array([reach] + counts)


def ragged_sizes(key, count, total, reach, skew):
    if count == 2:
        one = jax.random.randint(key, (), max(1, total - reach), min(reach, total - 1) + 1)
        return jnp.stack([one, total - one])
    sizes = jnp.asarray(profile(count, total, reach, skew), jnp.int32)
    pairs = (count - 1) // 2
    source_of, receiver = sizes[1:1 + 2 * pairs:2], sizes[2:2 + 2 * pairs:2]
    margin = jnp.minimum(source_of - 1, reach - receiver)
    moved = jax.random.randint(jax.random.fold_in(key, 1), (pairs,), 0, 1 << 20) % (margin + 1)
    sizes = sizes.at[1:1 + 2 * pairs:2].set(source_of - moved).at[2:2 + 2 * pairs:2].set(receiver + moved)
    return sizes[jax.random.permutation(jax.random.fold_in(key, 2), count)]


def gaussian(rng, dims, scale, limit, shards=(), kind=jnp.bfloat16):
    drawn = scale * jax.random.normal(rng, dims, jnp.float32)
    if shards:
        drawn = drawn * shard_levels(rng, dims, shards, -0.22, 0.18)
    return jnp.clip(drawn, -limit, limit).astype(kind)


def setup_inputs(seed: int = 0) -> dict:
    splits = jax.random.split(jax.random.key(seed), 10)
    queries = draw_queries(jax.random.fold_in(splits[9], 71), 0)
    keys_values = draw_keys_values(jax.random.fold_in(splits[9], 71), 0)
    out_grad = gaussian(splits[2], (BATCH, SEQ, Q_HEADS * HD), 1.0, 6.0, ((0, 4), (1, 16), (2, 8)))
    activations = gaussian(splits[3], (BATCH, SEQ, D), 1.0, 6.0, ((0, 4), (1, 16), (2, 8)))
    adapter_down = gaussian(splits[4], (3, RANK, D), D ** -0.5, 0.0625, ((2, 8),))
    adapter_up_q = gaussian(splits[5], (RANK, Q_HEADS * HD), (Q_HEADS * HD) ** -0.5, 0.0625, ((1, 8),))
    adapter_up_kv = gaussian(splits[6], (2, RANK, KV_HEADS * HD), (KV_HEADS * HD) ** -0.5, 0.1875, ((2, 8),))
    doc_lengths = jax.vmap(lambda own: ragged_sizes(own, DOCS, SEQ, DOC_MOST, 2))(jax.random.split(splits[7], BATCH)).reshape((BATCH, DOCS)).astype(jnp.int32)
    block_order = jax.random.permutation(splits[8], SLOTS).astype(jnp.int32)
    return dict(queries=queries, keys_values=keys_values, out_grad=out_grad, activations=activations, adapter_down=adapter_down, adapter_up_q=adapter_up_q, adapter_up_kv=adapter_up_kv, doc_lengths=doc_lengths, block_order=block_order)


neg_large = -1e+30
adapter_scale = 2.0

def round_low(values):
    return lax.optimization_barrier(values.astype(jnp.bfloat16)).astype(jnp.float32)

def sequence_layout(order, lengths):
    row_index = jnp.arange(SEQ, dtype=jnp.int32)
    slot_match = (row_index // BLOCK)[:, None] == jnp.arange(SLOTS, dtype=jnp.int32)[None, :]
    starts = lax.optimization_barrier(jnp.sum(jnp.where(slot_match, order[None, :], 0), axis=1)).astype(jnp.int32)
    positions = (starts * BLOCK + row_index % BLOCK).astype(jnp.int32)
    bounds = jnp.cumsum(lengths).astype(jnp.int32)
    documents = lax.optimization_barrier(jnp.sum((positions[:, None] >= bounds[None, :]).astype(jnp.int32), axis=1)).astype(jnp.int32)
    return (positions, documents)

def head_grads(items):
    query_tile, key_tile, value_tile, grad_out, positions, documents = items
    factor = 1.0 / math.sqrt(HD)
    query_full = query_tile.astype(jnp.float32)
    key_full = key_tile.astype(jnp.float32)
    value_full = value_tile.astype(jnp.float32)
    grad_full = grad_out.astype(jnp.float32)
    visible = (positions[None, :] <= positions[:, None]) & (documents[None, :] == documents[:, None])
    scores = jnp.einsum('rgd,nd->grn', query_full, key_full) * factor
    scores = jnp.where(visible[None], scores, neg_large)
    largest = lax.optimization_barrier(jnp.max(scores, axis=2, keepdims=True))
    weights = jnp.where(visible[None], jnp.exp(scores - largest), 0.0)
    probs = weights / lax.optimization_barrier(jnp.sum(weights, axis=2, keepdims=True))
    slopes = jnp.einsum('rgd,nd->grn', grad_full, value_full)
    mean_slope = lax.optimization_barrier(jnp.sum(probs * slopes, axis=2, keepdims=True))
    score_grads = round_low(probs * (slopes - mean_slope) * factor)
    probs_low = round_low(probs)
    grad_query = jnp.einsum('grn,nd->rgd', score_grads, key_full)
    score_parts = score_grads.reshape(GROUP, N_CTX, ROWS_DEV, SEQ)
    prob_parts = probs_low.reshape(GROUP, N_CTX, ROWS_DEV, SEQ)
    query_parts = query_full.reshape(N_CTX, ROWS_DEV, GROUP, HD)
    grad_parts = grad_full.reshape(N_CTX, ROWS_DEV, GROUP, HD)
    key_parts = round_low(jnp.einsum('gcrn,crgd->cnd', score_parts, query_parts))
    value_parts = round_low(jnp.einsum('gcrn,crgd->cnd', prob_parts, grad_parts))
    grad_pair = jnp.stack([lax.optimization_barrier(jnp.sum(key_parts, axis=0)), lax.optimization_barrier(jnp.sum(value_parts, axis=0))])
    return (grad_query, grad_pair)

def reference(queries, keys_values, out_grad, activations, adapter_down, adapter_up_q, adapter_up_kv, doc_lengths, block_order):
    positions, documents = jax.vmap(lambda lengths: sequence_layout(block_order, lengths))(doc_lengths)
    query_items = queries.reshape(BATCH, SEQ, KV_HEADS, GROUP, HD).transpose(0, 2, 1, 3, 4).reshape(BATCH * KV_HEADS, SEQ, GROUP, HD)
    grad_items = out_grad.reshape(BATCH, SEQ, KV_HEADS, GROUP, HD).transpose(0, 2, 1, 3, 4).reshape(BATCH * KV_HEADS, SEQ, GROUP, HD)
    pair_items = keys_values.reshape(2, BATCH, SEQ, KV_HEADS, HD).transpose(0, 1, 3, 2, 4).reshape(2, BATCH * KV_HEADS, SEQ, HD)
    position_items = jnp.repeat(positions, KV_HEADS, axis=0)
    document_items = jnp.repeat(documents, KV_HEADS, axis=0)
    grad_query, grad_pair = lax.map(head_grads, (query_items, pair_items[0], pair_items[1], grad_items, position_items, document_items))
    grad_queries = grad_query.reshape(BATCH, KV_HEADS, SEQ, GROUP, HD).transpose(0, 2, 1, 3, 4).reshape(BATCH, SEQ, Q_HEADS * HD).astype(jnp.bfloat16)
    grad_keys_values = grad_pair.reshape(BATCH, KV_HEADS, 2, SEQ, HD).transpose(2, 0, 3, 1, 4).reshape(2, BATCH, SEQ, KV_HEADS * HD).astype(jnp.bfloat16)
    x_full = activations.astype(jnp.float32)
    low_inputs = round_low(jnp.einsum('bld,jrd->jblr', x_full, adapter_down.astype(jnp.float32)))
    grad_q_full = grad_queries.astype(jnp.float32)
    grad_kv_full = grad_keys_values.astype(jnp.float32)
    up_kv_full = adapter_up_kv.astype(jnp.float32)
    low_grads = round_low(jnp.stack([jnp.einsum('blc,rc->blr', grad_q_full, adapter_up_q.astype(jnp.float32)), jnp.einsum('blc,rc->blr', grad_kv_full[0], up_kv_full[0]), jnp.einsum('blc,rc->blr', grad_kv_full[1], up_kv_full[1])]))
    norm = adapter_scale / math.sqrt(BATCH * SEQ)
    grad_down = norm * jnp.einsum('jblr,bld->jrd', low_grads, x_full)
    grad_up_q = norm * jnp.einsum('blr,blc->rc', low_inputs[0], grad_q_full)
    grad_up_kv = norm * jnp.einsum('jblr,jblc->jrc', low_inputs[1:], grad_kv_full)
    return (grad_queries, grad_keys_values, grad_down, grad_up_q, grad_up_kv)
```

```python
import functools
import math

import jax
import jax.numpy as jnp
from jax import lax
from jax.experimental import pallas as pl
from jax.experimental.pallas import tpu as pltpu
from jax.sharding import PartitionSpec as P

MESH = pl.DeviceIdType.MESH
BF16 = jnp.bfloat16
F32 = jnp.float32
VMEM = pltpu.VMEM
NT = (((1,), (1,)), ((), ()))
NN = (((1,), (0,)), ((), ()))
TN = (((0,), (0,)), ((), ()))
ADAPTER_SCALE = 2.0
NEG_LARGE = -1e30
TILE = 272


def dot(a, b, dims):
    return lax.dot_general(a, b, dims, preferred_element_type=F32)


def remote(src, dst, send_sem, recv_sem, device):
    return pltpu.make_async_remote_copy(
        src_ref=src,
        dst_ref=dst,
        send_sem=send_sem,
        recv_sem=recv_sem,
        device_id=device,
        device_id_type=MESH,
    )


def greet(devices):
    barrier = pltpu.get_barrier_semaphore()
    for device in devices:
        pl.semaphore_signal(barrier, inc=1, device_id=device, device_id_type=MESH)
    return barrier


def ring_order(steps):
    order = [(0, 0)]
    for s in range(1, steps):
        order += [(0, s), (1, s - 1)]
    return order + [(1, steps - 1)]


def gather_kernel(ys, kv_ref, out_ref, z_sems, send_sems, recv_sems):
    c = lax.axis_index("ctx")
    y, z = c % ys, c // ys
    far = ys // 2
    partner = (1 - z) * ys + y
    right = z * ys + (y + 1) % ys
    left = z * ys + (y + ys - 1) % ys
    barrier = greet([{"ctx": right}, {"ctx": left}, {"ctx": partner}])
    pl.semaphore_wait(barrier, 3)

    across = remote(
        kv_ref, out_ref.at[:, c], z_sems.at[0], z_sems.at[1], {"ctx": partner}
    )
    across.start()

    def hop(u, d, s, origin):
        slot = (z if u == 0 else 1 - z) * ys + origin % ys
        whole = out_ref.at[:, slot]
        dst = out_ref.at[d, slot] if s == far - 1 else whole
        src = kv_ref if (s == 0 and u == 0) else whole
        if s == far - 1:
            src = out_ref.at[d, slot]
        return remote(
            src, dst, send_sems.at[u, d, s], recv_sems.at[u, d, s],
            {"ctx": right if d == 0 else left},
        )

    def sent(u, d, s):
        return hop(u, d, s, y + ys - s if d == 0 else y + s)

    def landed(u, d, s):
        return hop(u, d, s, y + ys - 1 - s if d == 0 else y + 1 + s)

    for u, s in ring_order(far):
        if u == 1 and s == 0:
            across.wait_recv()
        for d in range(2):
            if s > 0:
                landed(u, d, s - 1).wait_recv()
            sent(u, d, s).start()
        if u == 0 and s == 0:
            out_ref[:, c] = kv_ref[...]
    for u in range(2):
        for d in range(2):
            landed(u, d, far - 1).wait_recv()
    across.wait_send()
    for u in range(2):
        for d in range(2):
            for s in range(far):
                sent(u, d, s).wait_send()


def attention_kernel(
    group, block, slots, docs,
    order_ref, lengths_ref, q_ref, g_ref, kv_ref, gq_ref, parts_ref,
    inverse, ks, vs, s_scr, p_scr, acc,
):
    pad = TILE
    head = q_ref.shape[1] // group
    lanes = group * block
    factor = 1.0 / math.sqrt(head)
    mine = lax.axis_index("ctx") * 2

    def invert(i, _):
        inverse[order_ref[i]] = i
        return 0

    lax.fori_loop(0, slots, invert, 0)
    ks[:pad] = jnp.zeros((pad, head), BF16)
    vs[:pad] = jnp.zeros((pad, head), BF16)

    def sort(p, _):
        slot = inverse[p]
        dst = pl.ds(pl.multiple_of(pad + p * block, 16), block)
        src = pl.ds(pl.multiple_of(slot * block, 16), block)
        ks[dst, :] = kv_ref[0, src, :]
        vs[dst, :] = kv_ref[1, src, :]
        return 0

    lax.fori_loop(0, slots, sort, 0)
    acc[...] = jnp.zeros(acc.shape, F32)

    lane = lax.broadcasted_iota(jnp.int32, (1, lanes), 1)
    row = lane
    for g in range(1, group):
        row = jnp.where(lane >= g * block, lane - g * block, row)
    sub = lax.broadcasted_iota(jnp.int32, (TILE, lanes), 0)

    for half in range(2):
        place = order_ref[mine + half]
        first = place * block
        pos = row + first
        begin = jnp.zeros((1, lanes), jnp.int32)
        begin_first = 0
        bound = 0
        for i in range(docs):
            bound = bound + lengths_ref[0, i]
            begin = jnp.where(pos >= bound, bound, begin)
            begin_first = jnp.where(first >= bound, bound, begin_first)
        end = first + block
        tiles = (end - begin_first + TILE - 1) // TILE
        rows = slice(half * block, (half + 1) * block)
        q = jnp.concatenate(
            [q_ref[rows, g * head : (g + 1) * head] for g in range(group)], axis=0
        )
        go = jnp.concatenate(
            [g_ref[rows, g * head : (g + 1) * head] for g in range(group)], axis=0
        )

        def keys_at(t):
            return pl.ds(pl.multiple_of(pad + end - (t + 1) * TILE, 16), TILE)

        def hold_at(t):
            return pl.ds(pl.multiple_of(t * TILE, 16), TILE)

        def score(t, most):
            at = end - (t + 1) * TILE
            s = dot(ks[keys_at(t), :], q, NT) * (factor * math.log2(math.e))
            seen = (sub >= begin - at) & (sub <= pos - at)
            s = jnp.where(seen, s, NEG_LARGE)
            s_scr[hold_at(t), :] = s
            return jnp.maximum(most, jnp.max(s.reshape(TILE // 8, 8, lanes), axis=0))

        most = lax.fori_loop(0, tiles, score, jnp.full((8, lanes), NEG_LARGE, F32))
        most = jnp.max(most, axis=0, keepdims=True)

        def weigh(t, sums):
            total, slope = sums
            w = jnp.exp2(s_scr[hold_at(t), :] - most)
            s_scr[hold_at(t), :] = w
            d = dot(vs[keys_at(t), :], go, NT)
            p_scr[hold_at(t), :] = d
            total = total + jnp.sum(w.reshape(TILE // 8, 8, lanes), axis=0)
            slope = slope + jnp.sum((w * d).reshape(TILE // 8, 8, lanes), axis=0)
            return total, slope

        zero = jnp.zeros((8, lanes), F32)
        total, slope = lax.fori_loop(0, tiles, weigh, (zero, zero))
        over = 1.0 / jnp.sum(total, axis=0, keepdims=True)
        mean = jnp.sum(slope, axis=0, keepdims=True) * over

        def grads(t, gq):
            prob = s_scr[hold_at(t), :] * over
            ds = (prob * (p_scr[hold_at(t), :] - mean)).astype(BF16)
            acc[1, keys_at(t), :] += dot(prob.astype(BF16), go, NN)
            acc[0, keys_at(t), :] += dot(ds, q, NN)
            return gq + dot(ks[keys_at(t), :], ds, TN)

        gq = lax.fori_loop(0, tiles, grads, jnp.zeros((head, lanes), F32))
        gq = (gq * factor).T.astype(BF16)
        for g in range(group):
            gq_ref[rows, g * head : (g + 1) * head] = gq[g * block : (g + 1) * block]

    def unsort(p, _):
        slot = inverse[p]
        src = pl.ds(pl.multiple_of(pad + p * block, 16), block)
        dst = pl.ds(pl.multiple_of(slot * block, 16), block)
        parts_ref[0, dst, :] = (acc[0, src, :] * factor).astype(BF16)
        parts_ref[1, dst, :] = acc[1, src, :].astype(BF16)
        return 0

    lax.fori_loop(0, slots, unsort, 0)


def reduce_kernel(
    ys, xs, heads, norm,
    parts_ref, gq_ref, act_ref, down_ref, upq_ref, upkv_ref,
    gkv_ref, gdown_ref, gupq_ref, gupkv_ref,
    slots, cross, low_a, low_b, y_out, y_in, g_in, a_in,
    ring_send, ring_recv, cross_sem, la_send, la_recv, lb_send, lb_recv,
    y_send, y_recv, g_send, g_recv, a_send, a_recv,
):
    dp, c, h = lax.axis_index("dp"), lax.axis_index("ctx"), lax.axis_index("head")
    y, z = c % ys, c // ys
    far = ys // 2
    rank = upq_ref.shape[0]
    group = 2 * xs
    partner = {"ctx": (1 - z) * ys + y}
    right = {"ctx": z * ys + (y + 1) % ys}
    left = {"ctx": z * ys + (y + ys - 1) % ys}
    y_peers = [{"ctx": z * ys + (y + k) % ys} for k in range(1, ys)]
    h_peers = [{"head": (h + k) % heads} for k in range(1, heads)]
    me_g = dp * 2 + z
    g_peers = []
    for k in range(1, group):
        other = (me_g + k) % group
        g_peers.append({"dp": other // 2, "ctx": (other % 2) * ys + y})

    barrier = greet(y_peers + h_peers + g_peers)

    act = act_ref[...]
    gq = gq_ref[...]
    low_a[h, : 3 * rank, :] = dot(down_ref[...], act, NT).astype(BF16)
    low_a[h, 3 * rank :, :] = dot(upq_ref[...], gq, NT).astype(BF16)
    pl.semaphore_wait(barrier, ys - 1 + heads - 1 + group - 1)

    def steps_of(j, d):
        return far if j == d else far - 1

    def target(j, d, s):
        away = steps_of(j, d) - s
        return (y + away) % ys if d == 0 else (y + ys - away) % ys

    def part(j, u, at):
        return parts_ref.at[j, ((1 - z) if u == 0 else z) * ys + at]

    def hop(j, d, u, s):
        src = part(j, u, target(j, d, 0)) if s == 0 else slots.at[j, d, u, s - 1]
        return remote(
            src, slots.at[j, d, u, s], ring_send.at[j, d, u, s],
            ring_recv.at[j, d, u, s], right if d == 0 else left,
        )

    def advance(u, s):
        for j in range(2):
            for d in range(2):
                if s >= steps_of(j, d):
                    continue
                if s > 0:
                    hop(j, d, u, s - 1).wait_recv()
                    here = slots[j, d, u, s - 1].astype(F32)
                    more = part(j, u, target(j, d, s))[...].astype(F32)
                    slots[j, d, u, s - 1] = (here + more).astype(BF16)
                hop(j, d, u, s).start()

    def finish(j, u):
        total = part(j, u, y)[...].astype(F32)
        for d in range(2):
            hop(j, d, u, steps_of(j, d) - 1).wait_recv()
            total = total + slots[j, d, u, steps_of(j, d) - 1].astype(F32)
        return total

    def cross_hop(j):
        return remote(
            cross.at[0, j], cross.at[1, j], cross_sem.at[0, j], cross_sem.at[1, j], partner
        )

    def spread(buffer, me, peers, size, send, recv):
        def one(k, slot):
            return remote(
                buffer.at[slot], buffer.at[slot], send.at[k], recv.at[k], peers[k]
            )

        def start():
            for k in range(size - 1):
                one(k, me).start()

        def arrive():
            for k in range(size - 1):
                one(k, (me + size - 1 - k) % size).wait_recv()

        def drain():
            for k in range(size - 1):
                one(k, me).wait_send()

        return start, arrive, drain

    def total_of(buffer, size):
        total = buffer[0].astype(F32)
        for k in range(1, size):
            total = total + buffer[k].astype(F32)
        return total

    la_start, la_arrive, la_drain = spread(low_a, h, h_peers, heads, la_send, la_recv)
    lb_start, lb_arrive, lb_drain = spread(low_b, h, h_peers, heads, lb_send, lb_recv)
    g_start, g_arrive, g_drain = spread(g_in, me_g, g_peers, group, g_send, g_recv)
    a_start, a_arrive, a_drain = spread(a_in, y, y_peers, ys, a_send, a_recv)

    order = ring_order(far)
    advance(*order[0])
    la_start()
    width = act.shape[1] // ys

    for i, (u, s) in enumerate(order[1:]):
        advance(u, s)
        if i == 2:
            la_arrive()
            low = total_of(low_a, heads).astype(BF16)
            first = dot(low[3 * rank :], act, NN).astype(BF16)
            second = dot(low[:rank], gq, NN).astype(BF16)
            for k in range(ys):
                y_out[k, :rank, :] = first[:, k * width : (k + 1) * width]
                y_out[k, rank : 2 * rank, :] = second[:, k * width : (k + 1) * width]
        if (u, s) == (0, far - 1):
            pass
    for j in range(2):
        cross[0, j] = finish(j, 0).astype(BF16)
        cross_hop(j).start()
    for j in range(2):
        total = finish(j, 1)
        cross_hop(j).wait_recv()
        gkv = (total + cross[1, j].astype(F32)).astype(BF16)
        gkv_ref[j] = gkv
        low_b[h, j * rank : (j + 1) * rank, :] = dot(upkv_ref[j], gkv, NT).astype(BF16)
    lb_start()
    for k in range(2, ys):
        y_out[k, 4 * rank :, :] = jnp.zeros((rank, width), BF16)
    for j in range(2):
        y_out[j, 4 * rank :, :] = dot(
            low[(1 + j) * rank : (2 + j) * rank], gkv_ref[j], NN
        ).astype(BF16)
    lb_arrive()
    low_kv = total_of(low_b, heads).astype(BF16)
    both = dot(low_kv, act, NN).astype(BF16)
    for k in range(ys):
        y_out[k, 2 * rank : 4 * rank, :] = both[:, k * width : (k + 1) * width]

    def y_hop(k, to, slot):
        return remote(y_out.at[to], y_in.at[slot], y_send.at[k], y_recv.at[k], y_peers[k])

    for k in range(ys - 1):
        y_hop(k, (y + 1 + k) % ys, y).start()
    y_in[y] = y_out[y]
    for k in range(ys - 1):
        y_hop(k, 0, (y + ys - 1 - k) % ys).wait_recv()
    g_in[me_g] = total_of(y_in, ys).astype(BF16)
    g_start()
    g_arrive()
    a_in[y] = (total_of(g_in, group) * norm).astype(BF16)
    a_start()
    a_arrive()
    for k in range(ys):
        piece = a_in[k].astype(F32)
        at = slice(k * width, (k + 1) * width)
        gdown_ref[:rank, at] = piece[:rank]
        gupq_ref[:, at] = piece[rank : 2 * rank]
        gdown_ref[rank:, at] = piece[2 * rank : 4 * rank]
        if k < 2:
            gupkv_ref[k] = piece[4 * rank :]

    la_drain()
    lb_drain()
    g_drain()
    a_drain()
    for k in range(ys - 1):
        y_hop(k, (y + 1 + k) % ys, y).wait_send()
    for j in range(2):
        cross_hop(j).wait_send()
        for d in range(2):
            for u in range(2):
                for s in range(steps_of(j, d)):
                    hop(j, d, u, s).wait_send()


def solution(mesh):
    contexts, heads, xs = mesh.shape["ctx"], mesh.shape["head"], mesh.shape["dp"]
    ys = contexts // 2
    vmem = pl.BlockSpec(memory_space=VMEM)
    smem = pl.BlockSpec(memory_space=pltpu.SMEM)
    dma = pltpu.SemaphoreType.DMA

    def on_device(q, kv, go, act, down, upq, upkv, lengths, order):
        rows, width = q.shape[1], q.shape[2]
        head = kv.shape[3]
        group = width // head
        seq = rows * contexts
        slots = order.shape[0]
        block = seq // slots
        docs = lengths.shape[1]
        rank = upq.shape[0]
        far = ys // 2
        most = ((seq // 2 + block) // TILE + 1) * TILE
        kv = kv.reshape(2, rows, head)
        q, go, act = q.reshape(rows, width), go.reshape(rows, width), act.reshape(rows, width)

        gathered = pl.pallas_call(
            functools.partial(gather_kernel, ys),
            out_shape=jax.ShapeDtypeStruct((2, contexts, rows, head), BF16),
            in_specs=[vmem],
            out_specs=vmem,
            scratch_shapes=[dma((2,)), dma((2, 2, far)), dma((2, 2, far))],
            compiler_params=pltpu.CompilerParams(
                collective_id=0, has_side_effects=True, vmem_limit_bytes=32 << 20
            ),
            name="gather_keys_values",
        )(kv)

        grad_q, parts = pl.pallas_call(
            functools.partial(attention_kernel, group, block, slots, docs),
            out_shape=(
                jax.ShapeDtypeStruct((rows, width), BF16),
                jax.ShapeDtypeStruct((2, seq, head), BF16),
            ),
            in_specs=[smem, smem, vmem, vmem, vmem],
            out_specs=(vmem, vmem),
            scratch_shapes=[
                pltpu.SMEM((slots,), jnp.int32),
                VMEM((TILE + seq, head), BF16),
                VMEM((TILE + seq, head), BF16),
                VMEM((most, group * block), F32),
                VMEM((most, group * block), F32),
                VMEM((2, TILE + seq, head), F32),
            ],
            compiler_params=pltpu.CompilerParams(vmem_limit_bytes=56 << 20),
            name="attention_grads",
        )(order, lengths, q, go, gathered.reshape(2, seq, head))

        width_y = width // ys
        norm = ADAPTER_SCALE / math.sqrt(xs * seq)
        gkv, gdown, gupq, gupkv = pl.pallas_call(
            functools.partial(reduce_kernel, ys, xs, heads, norm),
            out_shape=(
                jax.ShapeDtypeStruct((2, rows, head), BF16),
                jax.ShapeDtypeStruct((3 * rank, width), F32),
                jax.ShapeDtypeStruct((rank, width), F32),
                jax.ShapeDtypeStruct((2, rank, head), F32),
            ),
            in_specs=[vmem] * 6,
            out_specs=(vmem,) * 4,
            scratch_shapes=[
                VMEM((2, 2, 2, far, rows, head), BF16),
                VMEM((2, 2, rows, head), BF16),
                VMEM((heads, 4 * rank, rows), BF16),
                VMEM((heads, 2 * rank, rows), BF16),
                VMEM((ys, 5 * rank, width_y), BF16),
                VMEM((ys, 5 * rank, width_y), BF16),
                VMEM((2 * xs, 5 * rank, width_y), BF16),
                VMEM((ys, 5 * rank, width_y), BF16),
                dma((2, 2, 2, far)),
                dma((2, 2, 2, far)),
                dma((2, 2)),
                dma((heads - 1,)),
                dma((heads - 1,)),
                dma((heads - 1,)),
                dma((heads - 1,)),
                dma((ys - 1,)),
                dma((ys - 1,)),
                dma((2 * xs - 1,)),
                dma((2 * xs - 1,)),
                dma((ys - 1,)),
                dma((ys - 1,)),
            ],
            compiler_params=pltpu.CompilerParams(
                collective_id=1, has_side_effects=True, vmem_limit_bytes=48 << 20
            ),
            name="reduce_grads",
        )(
            parts.reshape(2, contexts, rows, head), grad_q, act,
            down.reshape(3 * rank, width), upq, upkv,
        )
        return (
            grad_q.reshape(1, rows, width),
            gkv.reshape(2, 1, rows, head),
            gdown.reshape(3, rank, width),
            gupq,
            gupkv,
        )

    return jax.shard_map(
        on_device,
        mesh=mesh,
        in_specs=(
            P("dp", "ctx", "head"),
            P(None, "dp", "ctx", "head"),
            P("dp", "ctx", "head"),
            P("dp", "ctx", "head"),
            P(None, None, "head"),
            P(None, "head"),
            P(None, None, "head"),
            P("dp", None),
            P(),
        ),
        out_specs=(
            P("dp", "ctx", "head"),
            P(None, "dp", "ctx", "head"),
            P(None, None, "head"),
            P(None, "head"),
            P(None, None, "head"),
        ),
        check_vma=False,
    )
```

```python
import functools
import math

import jax
import jax.numpy as jnp
from jax import lax
from jax.experimental import pallas as pl
from jax.experimental.pallas import tpu as pltpu
from jax.sharding import PartitionSpec as P

MESH = pl.DeviceIdType.MESH
BF16 = jnp.bfloat16
F32 = jnp.float32
VMEM = pltpu.VMEM
NT = (((1,), (1,)), ((), ()))
NN = (((1,), (0,)), ((), ()))
TN = (((0,), (0,)), ((), ()))
ADAPTER_SCALE = 2.0
NEG_LARGE = -1e30
BLOCK_LANES = 256
GATHER_LAG = 3


def dot(a, b, dims):
    return lax.dot_general(a, b, dims, preferred_element_type=F32)


def remote(src, dst, send_sem, recv_sem, device):
    return pltpu.make_async_remote_copy(
        src_ref=src,
        dst_ref=dst,
        send_sem=send_sem,
        recv_sem=recv_sem,
        device_id=device,
        device_id_type=MESH,
    )


def greet(devices):
    barrier = pltpu.get_barrier_semaphore()
    for device in devices:
        pl.semaphore_signal(barrier, inc=1, device_id=device, device_id_type=MESH)
    return barrier


def fused_kernel(
    ys, xs, heads, group, slots_n, docs, norm,
    order_ref, lengths_ref, q_ref, kv_ref, go_ref, act_ref, down_ref, upq_ref, upkv_ref,
    gq_ref, gkv_ref, sum_a, sum_b,
    kv_all, q_st, g_st, s_scr, p_scr, stats, limits, gq_t, own,
    ring_out, ring_in, cross, low_a, low_mine, low_other, low_q, low_kv_out, low_kv,
    ya_out, ya_in, yb_out, yb_in, ga_in, gb_in,
    z_sems, gather_send, gather_recv, ring_send, ring_recv, cross_send, cross_recv,
    la_send, la_recv, lo_sems, lq_send, lq_recv, lk_send, lk_recv, lz_send, lz_recv,
    ya_send, ya_recv, yb_send, yb_recv, ga_send, ga_recv, gb_send, gb_recv,
    aa_send, aa_recv, ab_send, ab_recv,
):
    dp, c, h = lax.axis_index("dp"), lax.axis_index("ctx"), lax.axis_index("head")
    y, z = c % ys, c // ys
    far = ys // 2
    contexts = 2 * ys
    rows, head = kv_ref.shape[1], kv_ref.shape[2]
    rank = upq_ref.shape[0]
    block = rows // 2
    lanes = group * rows
    team = 2 * xs
    factor = 1.0 / math.sqrt(head)
    pieces = lanes // BLOCK_LANES
    tall = rows // 8

    across = (1 - z) * ys + y
    partner = {"ctx": across}
    right = {"ctx": z * ys + (y + 1) % ys}
    left = {"ctx": z * ys + (y + ys - 1) % ys}
    y_peers = [{"ctx": z * ys + (y + k) % ys} for k in range(1, ys)]
    h_peers = [{"head": (h + k) % heads} for k in range(1, heads)]
    z_peers = [{"ctx": across, "head": (h + k) % heads} for k in range(heads)]
    me_t = dp * 2 + z
    t_peers = []
    for k in range(1, team):
        other = (me_t + k) % team
        t_peers.append({"dp": other // 2, "ctx": (other % 2) * ys + y})
    everyone = y_peers + h_peers + z_peers[1:] + t_peers
    barrier = greet(everyone)

    kv_all[:, c] = kv_ref[...]
    act = act_ref[...]
    low_a[h] = dot(down_ref[...], act, NT).astype(BF16)
    for g in range(group):
        q_st[g * rows : (g + 1) * rows] = q_ref[:, g * head : (g + 1) * head]
        g_st[g * rows : (g + 1) * rows] = go_ref[:, g * head : (g + 1) * head]
    lane = lax.broadcasted_iota(jnp.int32, (8, lanes), 1)
    row = lane
    for g in range(1, group):
        row = jnp.where(lane >= g * rows, lane - g * rows, row)
    first = order_ref[2 * c] * block
    second = order_ref[2 * c + 1] * block - block
    pos = row + jnp.where(row < block, first, second)
    begin = jnp.zeros((8, lanes), jnp.int32)
    bound = 0
    for i in range(docs):
        bound = bound + lengths_ref[0, i]
        begin = jnp.where(pos >= bound, bound, begin)
    limits[0] = begin
    limits[1] = pos
    stats[0] = jnp.full((8, lanes), NEG_LARGE, F32)
    stats[1] = jnp.zeros((8, lanes), F32)
    stats[2] = jnp.zeros((8, lanes), F32)
    gq_t[...] = jnp.zeros(gq_t.shape, F32)
    for u in range(2):
        ring_in[0, 1, u, far - 1] = jnp.zeros((rows, head), BF16)
        ring_in[1, 0, u, far - 1] = jnp.zeros((rows, head), BF16)
    pl.semaphore_wait(barrier, len(everyone))

    def spread(buffer, me, peers, size, send, recv):
        def one(k, slot):
            return remote(
                buffer.at[slot], buffer.at[slot], send.at[k], recv.at[k], peers[k]
            )

        def start():
            for k in range(size - 1):
                one(k, me).start()

        def arrive():
            for k in range(size - 1):
                one(k, (me + size - 1 - k) % size).wait_recv()

        def drain():
            for k in range(size - 1):
                one(k, me).wait_send()

        return start, arrive, drain

    def exchange(out, held, send, recv):
        def one(k, to, slot):
            return remote(out.at[to], held.at[slot], send.at[k], recv.at[k], y_peers[k])

        def start():
            for k in range(ys - 1):
                one(k, (y + 1 + k) % ys, y).start()
            held[y] = out[y]

        def arrive():
            for k in range(ys - 1):
                one(k, 0, (y + ys - 1 - k) % ys).wait_recv()

        def drain():
            for k in range(ys - 1):
                one(k, (y + 1 + k) % ys, y).wait_send()

        return start, arrive, drain

    def total_of(buffer, size):
        total = buffer[0].astype(F32)
        for k in range(1, size):
            total = total + buffer[k].astype(F32)
        return total

    cross_kv = remote(
        kv_all.at[:, c], kv_all.at[:, c], z_sems.at[0], z_sems.at[1], partner
    )
    cross_kv.start()

    def line(u):
        return (z + u * (1 - 2 * z)) * ys

    def hop(u, d, s, origin, half):
        slot = line(u) + (origin + ys) % ys
        ref = kv_all.at[d, slot] if half else kv_all.at[:, slot]
        return remote(
            ref, ref, gather_send.at[u, d, s], gather_recv.at[u, d, s],
            right if d == 0 else left,
        )

    def sent(u, d, s, half=False):
        return hop(u, d, s, y - s if d == 0 else y + s, half)

    def landed(u, d, s, half=False):
        return hop(u, d, s, y - 1 - s if d == 0 else y + 1 + s, half)

    for d in range(2):
        sent(0, d, 0).start()
    la_start, la_arrive, la_drain = spread(low_a, h, h_peers, heads, la_send, la_recv)
    la_start()

    sub = lax.broadcasted_iota(jnp.int32, (rows, BLOCK_LANES), 0)
    sub = sub.reshape(tall, 8, BLOCK_LANES)

    def score(slot):
        keys, values = kv_all[0, slot], kv_all[1, slot]
        upper = order_ref[2 * slot] * block
        lower = order_ref[2 * slot + 1] * block - block
        place = sub + jnp.where(sub < block, upper, lower)
        for i in range(pieces):
            at = slice(i * BLOCK_LANES, (i + 1) * BLOCK_LANES)
            s = dot(keys, q_st[at], NT) * (factor * math.log2(math.e))
            s = s.reshape(tall, 8, BLOCK_LANES)
            seen = (place >= limits[0, :, at]) & (place <= limits[1, :, at])
            s = jnp.where(seen, s, NEG_LARGE)
            s_scr[slot, :, at] = s.reshape(rows, BLOCK_LANES)
            d = dot(values, g_st[at], NT)
            p_scr[slot, :, at] = d
            before = stats[0, :, at]
            most = jnp.maximum(before, jnp.max(s, axis=0))
            w = jnp.exp2(s - most)
            shrink = jnp.exp2(before - most)
            stats[0, :, at] = most
            stats[1, :, at] = stats[1, :, at] * shrink + jnp.sum(w, axis=0)
            stats[2, :, at] = stats[2, :, at] * shrink + jnp.sum(
                w * d.reshape(tall, 8, BLOCK_LANES), axis=0
            )

    lag = GATHER_LAG

    def gather_step(k, carry):
        u = k % 2
        n = k // 2 - lag * u

        @pl.when((n >= 0) & (n < ys))
        def _():
            s = (n + 1) // 2
            d = (n + 1) % 2

            @pl.when((u == 1) & (n == 0))
            def _():
                cross_kv.wait_recv()
                for e in range(2):
                    sent(1, e, 0).start()

            @pl.when(((n + 1) % 2 == 0) & (s < far - 1))
            def _():
                for e in range(2):
                    landed(u, e, s - 1).wait_recv()
                    sent(u, e, s).start()

            @pl.when(((n + 1) % 2 == 0) & (s == far - 1))
            def _():
                for e in range(2):
                    landed(u, e, far - 2).wait_recv()
                    sent(u, e, far - 1, True).start()

            @pl.when(n == ys - 1)
            def _():
                for e in range(2):
                    landed(u, e, far - 1, True).wait_recv()

            score(line(u) + (y + 2 * ys + (2 * d - 1) * s) % ys)

        return carry

    lax.fori_loop(0, 2 * ys + 2 * lag, gather_step, 0)

    most = jnp.max(stats[0], axis=0, keepdims=True)
    shrink = jnp.exp2(stats[0] - most)
    total = jnp.sum(stats[1] * shrink, axis=0, keepdims=True)
    slope = jnp.sum(stats[2] * shrink, axis=0, keepdims=True)
    stats[0] = jnp.broadcast_to(most + jnp.log2(total), (8, lanes))
    stats[1] = jnp.broadcast_to(slope / total, (8, lanes))

    def ring(j, d, u, away, to):
        return remote(
            ring_out.at[j, d, u, away - 1], ring_in.at[j, d, u, away - 1],
            ring_send.at[j, d, u, away - 1], ring_recv.at[j, d, u, away - 1], to,
        )

    def reduce_step(k, carry):
        u = k % 2
        n = k // 2
        away = far - (n + 1) // 2
        d = (n + 1) % 2
        slot = line(1 - u) + (y + 2 * ys + (1 - 2 * d) * away) % ys
        keys = kv_all[0, slot]
        grad_k = jnp.zeros((rows, head), F32)
        grad_v = jnp.zeros((rows, head), F32)
        for i in range(pieces):
            at = slice(i * BLOCK_LANES, (i + 1) * BLOCK_LANES)
            s = s_scr[slot, :, at].reshape(tall, 8, BLOCK_LANES)
            prob = jnp.exp2(s - stats[0, :, at])
            tilt = p_scr[slot, :, at].reshape(tall, 8, BLOCK_LANES) - stats[1, :, at]
            ds = (prob * tilt).reshape(rows, BLOCK_LANES).astype(BF16)
            prob = prob.reshape(rows, BLOCK_LANES).astype(BF16)
            grad_v = grad_v + dot(prob, g_st[at], NN)
            grad_k = grad_k + dot(ds, q_st[at], NN)
            gq_t[:, at] += dot(keys, ds, TN)
        grads = (grad_k * factor, grad_v)

        @pl.when(n == 0)
        def _():
            for j in range(2):
                ring_out[j, j, u, far - 1] = grads[j].astype(BF16)
                ring(j, j, u, far, right if j == 0 else left).start()

        for e in range(2):

            @pl.when((n > 0) & (n < ys - 1) & (d == e))
            def _():
                to = right if e == 0 else left
                for j in (1 - e, e):
                    if j == e:
                        ring(j, e, u, away + 1, to).wait_recv()
                    else:

                        @pl.when(away < far - 1)
                        def _():
                            ring(j, e, u, away + 1, to).wait_recv()

                    more = ring_in[j, e, u, away].astype(F32)
                    ring_out[j, e, u, away - 1] = (grads[j] + more).astype(BF16)
                    ring(j, e, u, away, to).start()

        @pl.when(n == ys - 1)
        def _():
            for j in range(2):
                own[u, j] = grads[j]

        return carry

    lax.fori_loop(0, 2 * ys, reduce_step, 0)

    lq_start, lq_arrive, lq_drain = spread(low_q, h, h_peers, heads, lq_send, lq_recv)
    low_x = remote(
        low_mine.at[pl.ds(rank, 2 * rank)], low_other, lo_sems.at[0], lo_sems.at[1], partner
    )
    gq = (gq_t[...] * factor).T.astype(BF16)
    for g in range(group):
        gq_ref[:, g * head : (g + 1) * head] = gq[g * rows : (g + 1) * rows]
    gq = gq_ref[...]
    low_q[h] = dot(upq_ref[...], gq, NT).astype(BF16)
    lq_start()
    la_arrive()
    low = total_of(low_a, heads).astype(BF16)
    low_mine[...] = low
    low_x.start()
    width = act.shape[1] // ys

    def cut(buffer, at, value):
        value = value.astype(BF16)
        for k in range(ys):
            buffer[k, at : at + value.shape[0], :] = value[:, k * width : (k + 1) * width]

    cut(ya_out, rank, dot(low[:rank], gq, NN))

    ends = []
    for u in range(2):
        pair = []
        for j in range(2):
            total = own[u, j]
            for d in range(2):
                ring(j, d, u, 1, right if d == 0 else left).wait_recv()
                total = total + ring_in[j, d, u, 0].astype(F32)
            pair.append(total)
        ends.append(pair)
    cross_hops = [
        remote(cross.at[0, j], cross.at[1, j], cross_send.at[j], cross_recv.at[j], partner)
        for j in range(2)
    ]
    theirs = [ends[0][j].astype(BF16) for j in range(2)]
    ours = [ends[1][j].astype(BF16) for j in range(2)]
    for j in range(2):
        at = slice(j * rank, (j + 1) * rank)
        low_kv[z * heads + h, at, :] = dot(upkv_ref[j], ours[j], NT).astype(BF16)
        low_kv_out[at, :] = dot(upkv_ref[j], theirs[j], NT).astype(BF16)
    me_k = z * heads + h

    def same_hop(k, slot):
        return remote(
            low_kv.at[slot], low_kv.at[slot], lk_send.at[k], lk_recv.at[k], h_peers[k]
        )

    def other_hop(k, slot):
        return remote(low_kv_out, low_kv.at[slot], lz_send.at[k], lz_recv.at[k], z_peers[k])

    for k in range(heads):
        other_hop(k, me_k).start()
    for k in range(heads - 1):
        same_hop(k, me_k).start()
    for j in range(2):
        cross[0, j] = theirs[j]
        own[1, j] = ends[1][j]
        cross_hops[j].start()

    ya_start, ya_arrive, ya_drain = exchange(ya_out, ya_in, ya_send, ya_recv)
    yb_start, yb_arrive, yb_drain = exchange(yb_out, yb_in, yb_send, yb_recv)
    ga_start, ga_arrive, ga_drain = spread(ga_in, me_t, t_peers, team, ga_send, ga_recv)
    gb_start, gb_arrive, gb_drain = spread(gb_in, me_t, t_peers, team, gb_send, gb_recv)
    aa_start, aa_arrive, aa_drain = spread(sum_a, y, y_peers, ys, aa_send, aa_recv)
    ab_start, ab_arrive, ab_drain = spread(sum_b, y, y_peers, ys, ab_send, ab_recv)

    lq_arrive()
    cut(ya_out, 0, dot(total_of(low_q, heads).astype(BF16), act, NN))
    ya_start()
    low_x.wait_recv()
    yb_out[2:, 2 * rank :, :] = jnp.zeros((ys - 2, rank, width), BF16)
    for j in range(2):
        at = slice(j * rank, (j + 1) * rank)
        up = dot(low_mine[(1 + j) * rank : (2 + j) * rank], ours[j], NN)
        up = up + dot(low_other[at], theirs[j], NN)
        yb_out[j, 2 * rank :, :] = up.astype(BF16)
    for k in range(heads):
        other_hop(k, (1 - z) * heads + (h + heads - k) % heads).wait_recv()
    for k in range(heads - 1):
        same_hop(k, z * heads + (h + heads - 1 - k) % heads).wait_recv()
    cut(yb_out, 0, dot(total_of(low_kv, 2 * heads).astype(BF16), act, NN))
    yb_start()
    ya_arrive()
    ga_in[me_t] = total_of(ya_in, ys).astype(BF16)
    ga_start()
    yb_arrive()
    gb_in[me_t] = total_of(yb_in, ys).astype(BF16)
    gb_start()
    ga_arrive()
    sum_a[y] = (total_of(ga_in, team) * norm).astype(BF16)
    aa_start()
    gb_arrive()
    sum_b[y] = (total_of(gb_in, team) * norm).astype(BF16)
    ab_start()
    for j in range(2):
        cross_hops[j].wait_recv()
        gkv_ref[j] = (own[1, j] + cross[1, j].astype(F32)).astype(BF16)
    la_drain()
    lq_drain()
    ya_drain()
    yb_drain()
    ga_drain()
    gb_drain()
    low_x.wait_send()
    cross_kv.wait_send()
    for k in range(heads):
        other_hop(k, me_k).wait_send()
    for k in range(heads - 1):
        same_hop(k, me_k).wait_send()
    for u in range(2):
        for d in range(2):
            for s in range(far):
                sent(u, d, s, s == far - 1).wait_send()
    for j in range(2):
        cross_hops[j].wait_send()
        for d in range(2):
            for u in range(2):
                for away in range(1, far + (j == d)):
                    ring(j, d, u, away, right if d == 0 else left).wait_send()
    aa_arrive()
    ab_arrive()
    aa_drain()
    ab_drain()


def unpack_kernel(
    ys, rank, sum_a, sum_b, gq_in, gkv_in, gq_ref, gkv_ref, gdown_ref, gupq_ref, gupkv_ref
):
    gq_ref[...] = gq_in[...]
    gkv_ref[...] = gkv_in[...]
    width = sum_a.shape[2]
    for k in range(ys):
        at = slice(k * width, (k + 1) * width)
        gdown_ref[:rank, at] = sum_a[k, :rank].astype(F32)
        gupq_ref[:, at] = sum_a[k, rank:].astype(F32)
        gdown_ref[rank:, at] = sum_b[k, : 2 * rank].astype(F32)
    for j in range(2):
        gupkv_ref[j] = sum_b[j, 2 * rank :].astype(F32)


def solution(mesh):
    contexts, heads, xs = mesh.shape["ctx"], mesh.shape["head"], mesh.shape["dp"]
    ys = contexts // 2
    team = 2 * xs
    vmem = pl.BlockSpec(memory_space=VMEM)
    smem = pl.BlockSpec(memory_space=pltpu.SMEM)
    dma = pltpu.SemaphoreType.DMA

    def on_device(q, kv, go, act, down, upq, upkv, lengths, order):
        rows, width = q.shape[1], q.shape[2]
        head = kv.shape[3]
        group = width // head
        lanes = group * rows
        seq = rows * contexts
        slots = order.shape[0]
        docs = lengths.shape[1]
        rank = upq.shape[0]
        far = ys // 2
        kv = kv.reshape(2, rows, head)
        q, go, act = q.reshape(rows, width), go.reshape(rows, width), act.reshape(rows, width)
        wide = width // ys
        norm = ADAPTER_SCALE / math.sqrt(xs * seq)

        grad_q, grad_kv, sum_a, sum_b = pl.pallas_call(
            functools.partial(fused_kernel, ys, xs, heads, group, slots, docs, norm),
            out_shape=(
                jax.ShapeDtypeStruct((rows, width), BF16),
                jax.ShapeDtypeStruct((2, rows, head), BF16),
                jax.ShapeDtypeStruct((ys, 2 * rank, wide), BF16),
                jax.ShapeDtypeStruct((ys, 3 * rank, wide), BF16),
            ),
            in_specs=[smem, smem] + [vmem] * 7,
            out_specs=(vmem,) * 4,
            scratch_shapes=[
                VMEM((2, contexts, rows, head), BF16),
                VMEM((lanes, head), BF16),
                VMEM((lanes, head), BF16),
                VMEM((contexts, rows, lanes), F32),
                VMEM((contexts, rows, lanes), F32),
                VMEM((3, 8, lanes), F32),
                VMEM((2, 8, lanes), jnp.int32),
                VMEM((head, lanes), F32),
                VMEM((2, 2, rows, head), F32),
                VMEM((2, 2, 2, far, rows, head), BF16),
                VMEM((2, 2, 2, far, rows, head), BF16),
                VMEM((2, 2, rows, head), BF16),
                VMEM((heads, 3 * rank, rows), BF16),
                VMEM((3 * rank, rows), BF16),
                VMEM((2 * rank, rows), BF16),
                VMEM((heads, rank, rows), BF16),
                VMEM((2 * rank, rows), BF16),
                VMEM((2 * heads, 2 * rank, rows), BF16),
                VMEM((ys, 2 * rank, wide), BF16),
                VMEM((ys, 2 * rank, wide), BF16),
                VMEM((ys, 3 * rank, wide), BF16),
                VMEM((ys, 3 * rank, wide), BF16),
                VMEM((team, 2 * rank, wide), BF16),
                VMEM((team, 3 * rank, wide), BF16),
                dma((2,)),
                dma((2, 2, far)),
                dma((2, 2, far)),
                dma((2, 2, 2, far)),
                dma((2, 2, 2, far)),
                dma((2,)),
                dma((2,)),
                dma((heads - 1,)),
                dma((heads - 1,)),
                dma((2,)),
                dma((heads - 1,)),
                dma((heads - 1,)),
                dma((heads - 1,)),
                dma((heads - 1,)),
                dma((heads,)),
                dma((heads,)),
            ]
            + [dma((ys - 1,))] * 4
            + [dma((team - 1,))] * 4
            + [dma((ys - 1,))] * 4,
            compiler_params=pltpu.CompilerParams(
                collective_id=0, has_side_effects=True, vmem_limit_bytes=56 << 20
            ),
            name="attention_and_adapter_grads",
        )(order, lengths, q, kv, go, act, down.reshape(3 * rank, width), upq, upkv)

        gq, gkv, gdown, gupq, gupkv = pl.pallas_call(
            functools.partial(unpack_kernel, ys, rank),
            out_shape=(
                jax.ShapeDtypeStruct((rows, width), BF16),
                jax.ShapeDtypeStruct((2, rows, head), BF16),
                jax.ShapeDtypeStruct((3 * rank, width), F32),
                jax.ShapeDtypeStruct((rank, width), F32),
                jax.ShapeDtypeStruct((2, rank, head), F32),
            ),
            in_specs=[vmem] * 4,
            out_specs=(vmem,) * 5,
            name="write_outputs",
        )(sum_a, sum_b, grad_q, grad_kv)
        return (
            gq.reshape(1, rows, width),
            gkv.reshape(2, 1, rows, head),
            gdown.reshape(3, rank, width),
            gupq,
            gupkv,
        )

    return jax.shard_map(
        on_device,
        mesh=mesh,
        in_specs=(
            P("dp", "ctx", "head"),
            P(None, "dp", "ctx", "head"),
            P("dp", "ctx", "head"),
            P("dp", "ctx", "head"),
            P(None, None, "head"),
            P(None, "head"),
            P(None, None, "head"),
            P("dp", None),
            P(),
        ),
        out_specs=(
            P("dp", "ctx", "head"),
            P(None, "dp", "ctx", "head"),
            P(None, None, "head"),
            P(None, "head"),
            P(None, None, "head"),
        ),
        check_vma=False,
    )
```

```python
import functools
import math

import jax
import jax.numpy as jnp
from jax import lax
from jax.experimental import pallas as pl
from jax.experimental.pallas import tpu as pltpu
from jax.sharding import PartitionSpec as P

MESH = pl.DeviceIdType.MESH
BF16 = jnp.bfloat16
F32 = jnp.float32
VMEM = pltpu.VMEM
NT = (((1,), (1,)), ((), ()))
NN = (((1,), (0,)), ((), ()))
TN = (((0,), (0,)), ((), ()))
ADAPTER_SCALE = 2.0
NEG_LARGE = -1e30
BLOCK_LANES = 256
GATHER_LAG = 2


def dot(a, b, dims):
    return lax.dot_general(a, b, dims, preferred_element_type=F32)


def remote(src, dst, send_sem, recv_sem, device):
    return pltpu.make_async_remote_copy(
        src_ref=src,
        dst_ref=dst,
        send_sem=send_sem,
        recv_sem=recv_sem,
        device_id=device,
        device_id_type=MESH,
    )


def greet(devices):
    barrier = pltpu.get_barrier_semaphore()
    for device in devices:
        pl.semaphore_signal(barrier, inc=1, device_id=device, device_id_type=MESH)
    return barrier


def farthest(size):
    return sorted(range(size - 1), key=lambda k: -min(k + 1, size - 1 - k))


def fused_kernel(
    ys, xs, heads, group, slots_n, docs, norm,
    order_ref, lengths_ref, q_ref, kv_ref, go_ref, act_ref, down_ref, upq_ref, upkv_ref,
    gq_ref, gkv_ref, sum_a, sum_b,
    kv_all, q_st, g_st, act_v, s_scr, p_scr, stats, limits, gq_t, own, gq_v,
    ring_out, ring_in, cross, low_a, low_a2, low_mine, low_other, low_q, low_q2,
    low_kv, low_kv_out, low_kv2, ya_out, ya_in, yb_out, yb_in, ga_in, gb_in,
    in_sems, out_sem, z_sems, gather_send, gather_recv, ring_send, ring_recv, cross_send, cross_recv,
    la_send, la_recv, la2_send, la2_recv, lo_sems, lq_send, lq_recv, lq2_send, lq2_recv,
    lk_send, lk_recv, lk2_send, lk2_recv, lz_send, lz_recv,
    ya_send, ya_recv, yb_send, yb_recv, ga_send, ga_recv, gb_send, gb_recv,
    aa_send, aa_recv, ab_send, ab_recv,
):
    dp, c, h = lax.axis_index("dp"), lax.axis_index("ctx"), lax.axis_index("head")
    y, z = c % ys, c // ys
    far = ys // 2
    contexts = 2 * ys
    rows, head = kv_ref.shape[1], kv_ref.shape[2]
    rank = upq_ref.shape[0]
    block = rows // 2
    lanes = group * rows
    team = 2 * xs
    factor = 1.0 / math.sqrt(head)
    pieces = lanes // BLOCK_LANES
    tall = rows // 8

    across = (1 - z) * ys + y
    partner = {"ctx": across}
    right = {"ctx": z * ys + (y + 1) % ys}
    left = {"ctx": z * ys + (y + ys - 1) % ys}
    y_peers = [{"ctx": z * ys + (y + k) % ys} for k in range(1, ys)]
    chips = heads // 2
    core, chip = h % 2, h // 2
    pair_peers = [{"head": chip * 2 + 1 - core}]
    chip_heads = [(chip + k) % chips * 2 + core for k in range(chips)]
    chip_peers = [{"head": other} for other in chip_heads[1:]]
    z_peers = [{"ctx": across, "head": other} for other in chip_heads]
    me_t = dp * 2 + z
    t_peers = []
    for k in range(1, team):
        other = (me_t + k) % team
        t_peers.append({"dp": other // 2, "ctx": (other % 2) * ys + y})
    everyone = y_peers + pair_peers + chip_peers + z_peers[1:] + t_peers
    barrier = greet(everyone)
    kv_copy = pltpu.make_async_copy(kv_ref, kv_all.at[:, c], in_sems.at[2, 0])
    act_copy = pltpu.make_async_copy(act_ref, act_v, in_sems.at[2, 1])
    kv_copy.start()
    act_copy.start()
    copies = []
    for g in range(group):
        to = pl.ds(g * rows, rows)
        of = pl.ds(g * head, head)
        copies.append(pltpu.make_async_copy(q_ref.at[:, of], q_st.at[to], in_sems.at[0, g]))
        copies.append(pltpu.make_async_copy(go_ref.at[:, of], g_st.at[to], in_sems.at[1, g]))
    for copy in copies:
        copy.start()

    kv_copy.wait()
    pl.semaphore_wait(barrier, len(everyone))

    def spread(buffer, me, peers, size, send, recv):
        def one(k, slot):
            return remote(
                buffer.at[slot], buffer.at[slot], send.at[k], recv.at[k], peers[k]
            )

        def start():
            for k in farthest(size):
                one(k, me).start()

        def arrive():
            for k in range(size - 1):
                one(k, (me + size - 1 - k) % size).wait_recv()

        def drain():
            for k in range(size - 1):
                one(k, me).wait_send()

        return start, arrive, drain

    def exchange(out, held, send, recv):
        def one(k, to, slot):
            return remote(out.at[to], held.at[slot], send.at[k], recv.at[k], y_peers[k])

        def start():
            for k in farthest(ys):
                one(k, (y + 1 + k) % ys, y).start()
            held[y] = out[y]

        def arrive():
            for k in range(ys - 1):
                one(k, 0, (y + ys - 1 - k) % ys).wait_recv()

        def drain():
            for k in range(ys - 1):
                one(k, (y + 1 + k) % ys, y).wait_send()

        return start, arrive, drain

    def total_of(buffer, size):
        total = buffer[0].astype(F32)
        for k in range(1, size):
            total = total + buffer[k].astype(F32)
        return total

    cross_kv = remote(
        kv_all.at[:, c], kv_all.at[:, c], z_sems.at[0], z_sems.at[1], partner
    )
    cross_kv.start()

    def line(u):
        return (z + u * (1 - 2 * z)) * ys

    def hop(u, d, a, j, here):
        slot = line(u) + (y + 2 * ys + (2 * d - 1) * here) % ys
        whole = False
        ref = kv_all.at[:, slot] if whole else kv_all.at[j, slot]
        away = 1
        to = (y + away) % ys if d == 0 else (y + ys - away) % ys
        return remote(
            ref, ref, gather_send.at[u, d, a - 1, j], gather_recv.at[u, d, a - 1, j],
            {"ctx": z * ys + to},
        )

    def sent(u, d, a, j):
        return hop(u, d, a, j, a - 1)

    def landed(u, d, a, j):
        return hop(u, d, a, j, a)

    def messages(u, a):
        if a == far:
            return [(d, d) for d in range(2)]
        return [(d, j) for j in range(2) for d in range(2)]

    for d, j in messages(0, 1):
        sent(0, d, 1, j).start()
    la_start, la_arrive, la_drain = spread(low_a, core, pair_peers, 2, la_send, la_recv)
    la2_start, la2_arrive, la2_drain = spread(
        low_a2, chip, chip_peers, chips, la2_send, la2_recv
    )
    act_copy.wait()
    act = act_v[...]
    low_a[core] = dot(down_ref[...], act, NT).astype(BF16)
    la_start()
    lane = lax.broadcasted_iota(jnp.int32, (8, lanes), 1)
    row = lane
    for g in range(1, group):
        row = jnp.where(lane >= g * rows, lane - g * rows, row)
    first = order_ref[2 * c] * block
    second = order_ref[2 * c + 1] * block - block
    pos = row + jnp.where(row < block, first, second)
    begin = jnp.zeros((8, lanes), jnp.int32)
    bound = 0
    for i in range(docs):
        bound = bound + lengths_ref[0, i]
        begin = jnp.where(pos >= bound, bound, begin)
    limits[0] = begin
    limits[1] = pos
    stats[0] = jnp.full((8, lanes), NEG_LARGE, F32)
    stats[1] = jnp.zeros((8, lanes), F32)
    stats[2] = jnp.zeros((8, lanes), F32)
    gq_t[...] = jnp.zeros(gq_t.shape, F32)
    for copy in copies:
        copy.wait()
    for u in range(2):
        ring_in[0, 1, u, far - 1] = jnp.zeros((rows, head), BF16)
        ring_in[1, 0, u, far - 1] = jnp.zeros((rows, head), BF16)
    sub = lax.broadcasted_iota(jnp.int32, (rows, BLOCK_LANES), 0)
    sub = sub.reshape(tall, 8, BLOCK_LANES)

    def score(slot):
        keys, values = kv_all[0, slot], kv_all[1, slot]
        upper = order_ref[2 * slot] * block
        lower = order_ref[2 * slot + 1] * block - block
        place = sub + jnp.where(sub < block, upper, lower)
        for i in range(pieces):
            at = slice(i * BLOCK_LANES, (i + 1) * BLOCK_LANES)
            s = dot(keys, q_st[at], NT) * (factor * math.log2(math.e))
            s = s.reshape(tall, 8, BLOCK_LANES)
            seen = (place >= limits[0, :, at]) & (place <= limits[1, :, at])
            s = jnp.where(seen, s, NEG_LARGE)
            s_scr[slot, :, at] = s.reshape(rows, BLOCK_LANES)
            d = dot(values, g_st[at], NT)
            p_scr[slot, :, at] = d
            before = stats[0, :, at]
            most = jnp.maximum(before, jnp.max(s, axis=0))
            w = jnp.exp2(s - most)
            shrink = jnp.exp2(before - most)
            stats[0, :, at] = most
            stats[1, :, at] = stats[1, :, at] * shrink + jnp.sum(w, axis=0)
            stats[2, :, at] = stats[2, :, at] * shrink + jnp.sum(
                w * d.reshape(tall, 8, BLOCK_LANES), axis=0
            )

    lag = GATHER_LAG

    def gather_step(k, carry):
        u = k % 2
        n = k // 2 - lag * u
        s = (n + 1) // 2
        d = (n + 1) % 2

        for a in range(1, far + 1):

            @pl.when(k == 2 * (2 * a - 1))
            def _():
                for e, j in messages(0, a):
                    landed(0, e, a, j).wait_recv()
                    if a + 1 < far or (a + 1 == far and e == j):
                        sent(0, e, a + 1, j).start()

        @pl.when(k == 5)
        def _():
            cross_kv.wait_recv()
            for e, j in messages(1, 1):
                sent(1, e, 1, j).start()

        @pl.when(k == 7)
        def _():
            la_arrive()
            low_a2[chip] = total_of(low_a, 2).astype(BF16)
            la2_start()

        for a, at in ((1, 1), (2, 3), (3, 5), (4, 7)):

            @pl.when(k == 2 * (at + lag) + 1)
            def _():
                for e, j in messages(1, a):
                    landed(1, e, a, j).wait_recv()
                    if a + 1 < far or (a + 1 == far and e == j):
                        sent(1, e, a + 1, j).start()

        @pl.when((n >= 0) & (n < ys))
        def _():
            swap = 0
            score(line(u) + (y + 2 * ys + (2 * d - 1) * (s + swap)) % ys)

        return carry

    lax.fori_loop(0, 2 * ys + 2 * lag, gather_step, 0)

    most = jnp.max(stats[0], axis=0, keepdims=True)
    shrink = jnp.exp2(stats[0] - most)
    total = jnp.sum(stats[1] * shrink, axis=0, keepdims=True)
    slope = jnp.sum(stats[2] * shrink, axis=0, keepdims=True)
    stats[0] = jnp.broadcast_to(most + jnp.log2(total), (8, lanes))
    stats[1] = jnp.broadcast_to(slope / total, (8, lanes))

    def ring(j, d, u, away, to):
        return remote(
            ring_out.at[j, d, u, away - 1], ring_in.at[j, d, u, away - 1],
            ring_send.at[j, d, u, away - 1], ring_recv.at[j, d, u, away - 1], to,
        )

    low_x = remote(
        low_mine.at[pl.ds(rank, 2 * rank)], low_other, lo_sems.at[0], lo_sems.at[1], partner
    )

    def reduce_step(k, carry):
        u = k % 2
        n = k // 2
        away = far - (n + 1) // 2
        d = (n + 1) % 2
        slot = line(1 - u) + (y + 2 * ys + (1 - 2 * d) * away) % ys
        keys = kv_all[0, slot]
        grad_k = jnp.zeros((rows, head), F32)
        grad_v = jnp.zeros((rows, head), F32)
        for i in range(pieces):
            at = slice(i * BLOCK_LANES, (i + 1) * BLOCK_LANES)
            s = s_scr[slot, :, at].reshape(tall, 8, BLOCK_LANES)
            prob = jnp.exp2(s - stats[0, :, at])
            tilt = p_scr[slot, :, at].reshape(tall, 8, BLOCK_LANES) - stats[1, :, at]
            ds = (prob * tilt).reshape(rows, BLOCK_LANES).astype(BF16)
            prob = prob.reshape(rows, BLOCK_LANES).astype(BF16)
            grad_v = grad_v + dot(prob, g_st[at], NN)
            grad_k = grad_k + dot(ds, q_st[at], NN)
            gq_t[:, at] += dot(keys, ds, TN)
        grads = (grad_k * factor, grad_v)

        @pl.when(k == 3)
        def _():
            la2_arrive()
            low_mine[...] = total_of(low_a2, chips).astype(BF16)
            low_x.start()

        @pl.when(n == 0)
        def _():
            for j in range(2):
                ring_out[j, j, u, far - 1] = grads[j].astype(BF16)
                ring(j, j, u, far, right if j == 0 else left).start()

        for e in range(2):

            @pl.when((n > 0) & (n < ys - 1) & (d == e))
            def _():
                to = right if e == 0 else left
                for j in (1 - e, e):
                    if j == e:
                        ring(j, e, u, away + 1, to).wait_recv()
                    else:

                        @pl.when(away < far - 1)
                        def _():
                            ring(j, e, u, away + 1, to).wait_recv()

                    more = ring_in[j, e, u, away].astype(F32)
                    ring_out[j, e, u, away - 1] = (grads[j] + more).astype(BF16)
                    ring(j, e, u, away, to).start()

        @pl.when(n == ys - 1)
        def _():
            for j in range(2):
                own[u, j] = grads[j]

        return carry

    lax.fori_loop(0, 2 * ys, reduce_step, 0)

    lq_start, lq_arrive, lq_drain = spread(low_q, core, pair_peers, 2, lq_send, lq_recv)
    lq2_start, lq2_arrive, lq2_drain = spread(
        low_q2, chip, chip_peers, chips, lq2_send, lq2_recv
    )
    lk_start, lk_arrive, lk_drain = spread(low_kv, core, pair_peers, 2, lk_send, lk_recv)
    gq = (gq_t[...] * factor).T.astype(BF16)
    for g in range(group):
        gq_v[:, g * head : (g + 1) * head] = gq[g * rows : (g + 1) * rows]
    gq_copy = pltpu.make_async_copy(gq_v, gq_ref, out_sem)
    gq_copy.start()
    gq = gq_v[...]
    low_q[core] = dot(upq_ref[...], gq, NT).astype(BF16)
    lq_start()
    low = low_mine[...]
    width = act.shape[1] // ys

    def cut(buffer, at, value):
        value = value.astype(BF16)
        for k in range(ys):
            buffer[k, at : at + value.shape[0], :] = value[:, k * width : (k + 1) * width]

    cut(ya_out, rank, dot(low[:rank], gq, NN))

    lq_arrive()
    low_q2[chip] = total_of(low_q, 2).astype(BF16)
    lq2_start()

    ends = []
    for u in range(2):
        pair = []
        for j in range(2):
            total = own[u, j]
            for d in range(2):
                ring(j, d, u, 1, right if d == 0 else left).wait_recv()
                total = total + ring_in[j, d, u, 0].astype(F32)
            pair.append(total)
        ends.append(pair)
    cross_hops = [
        remote(cross.at[0, j], cross.at[1, j], cross_send.at[j], cross_recv.at[j], partner)
        for j in range(2)
    ]
    theirs = [ends[0][j].astype(BF16) for j in range(2)]
    ours = [ends[1][j].astype(BF16) for j in range(2)]
    for j in range(2):
        at = slice(j * rank, (j + 1) * rank)
        low_kv[core, 0, at, :] = dot(upkv_ref[j], ours[j], NT).astype(BF16)
        low_kv[core, 1, at, :] = dot(upkv_ref[j], theirs[j], NT).astype(BF16)
    lk_start()
    me_k = z * chips + chip

    def same_hop(k, slot):
        return remote(
            low_kv2.at[slot], low_kv2.at[slot], lk2_send.at[k], lk2_recv.at[k], chip_peers[k]
        )

    def other_hop(k, slot):
        return remote(low_kv_out, low_kv2.at[slot], lz_send.at[k], lz_recv.at[k], z_peers[k])

    for j in range(2):
        cross[0, j] = theirs[j]
        own[1, j] = ends[1][j]
    low_x.wait_recv()
    ya_out[2:, 2 * rank :, :] = jnp.zeros((ys - 2, rank, width), BF16)
    for j in range(2):
        at = slice(j * rank, (j + 1) * rank)
        up = dot(low_mine[(1 + j) * rank : (2 + j) * rank], ours[j], NN)
        up = up + dot(low_other[at], theirs[j], NN)
        ya_out[j, 2 * rank :, :] = up.astype(BF16)
    lk_arrive()
    low_kv2[me_k] = (low_kv[0, 0].astype(F32) + low_kv[1, 0].astype(F32)).astype(BF16)
    low_kv_out[...] = (low_kv[0, 1].astype(F32) + low_kv[1, 1].astype(F32)).astype(BF16)
    for k in range(chips):
        other_hop(k, me_k).start()
    for k in range(chips - 1):
        same_hop(k, me_k).start()

    ya_start, ya_arrive, ya_drain = exchange(ya_out, ya_in, ya_send, ya_recv)
    yb_start, yb_arrive, yb_drain = exchange(yb_out, yb_in, yb_send, yb_recv)
    ga_start, ga_arrive, ga_drain = spread(ga_in, me_t, t_peers, team, ga_send, ga_recv)
    gb_start, gb_arrive, gb_drain = spread(gb_in, me_t, t_peers, team, gb_send, gb_recv)
    aa_start, aa_arrive, aa_drain = spread(sum_a, y, y_peers, ys, aa_send, aa_recv)
    ab_start, ab_arrive, ab_drain = spread(sum_b, y, y_peers, ys, ab_send, ab_recv)

    lq2_arrive()
    cut(ya_out, 0, dot(total_of(low_q2, chips).astype(BF16), act, NN))
    ya_start()
    for k in range(chips):
        other_hop(k, (1 - z) * chips + (chip + chips - k) % chips).wait_recv()
    for k in range(chips - 1):
        same_hop(k, z * chips + (chip + chips - 1 - k) % chips).wait_recv()
    cut(yb_out, 0, dot(total_of(low_kv2, 2 * chips).astype(BF16), act, NN))
    yb_start()
    ya_arrive()
    ga_in[me_t] = total_of(ya_in, ys).astype(BF16)
    ga_start()
    yb_arrive()
    gb_in[me_t] = total_of(yb_in, ys).astype(BF16)
    gb_start()
    ga_arrive()
    sum_a[y] = (total_of(ga_in, team) * norm).astype(BF16)
    aa_start()
    gb_arrive()
    sum_b[y] = (total_of(gb_in, team) * norm).astype(BF16)
    ab_start()
    for j in range(2):
        cross_hops[j].start()
    for j in range(2):
        cross_hops[j].wait_recv()
        gkv_ref[j] = (own[1, j] + cross[1, j].astype(F32)).astype(BF16)
    la_drain()
    la2_drain()
    lq_drain()
    lq2_drain()
    lk_drain()
    ya_drain()
    yb_drain()
    ga_drain()
    gb_drain()
    low_x.wait_send()
    cross_kv.wait_send()
    for k in range(chips):
        other_hop(k, me_k).wait_send()
    for k in range(chips - 1):
        same_hop(k, me_k).wait_send()
    for u in range(2):
        for a in range(1, far + 1):
            for d, j in messages(u, a):
                sent(u, d, a, j).wait_send()
    for j in range(2):
        cross_hops[j].wait_send()
        for d in range(2):
            for u in range(2):
                for away in range(1, far + (j == d)):
                    ring(j, d, u, away, right if d == 0 else left).wait_send()
    aa_arrive()
    ab_arrive()
    aa_drain()
    ab_drain()
    gq_copy.wait()


def unpack_kernel(
    ys, rank, sum_a, sum_b, gq_in, gkv_in, gq_ref, gkv_ref, gdown_ref, gupq_ref, gupkv_ref
):
    gq_ref[...] = gq_in[...]
    gkv_ref[...] = gkv_in[...]
    width = sum_a.shape[2]
    for k in range(ys):
        at = slice(k * width, (k + 1) * width)
        gdown_ref[:rank, at] = sum_a[k, :rank].astype(F32)
        gupq_ref[:, at] = sum_a[k, rank : 2 * rank].astype(F32)
        gdown_ref[rank:, at] = sum_b[k].astype(F32)
    for j in range(2):
        gupkv_ref[j] = sum_a[j, 2 * rank :].astype(F32)


def solution(mesh):
    contexts, heads, xs = mesh.shape["ctx"], mesh.shape["head"], mesh.shape["dp"]
    ys = contexts // 2
    team, chips = 2 * xs, heads // 2
    vmem = pl.BlockSpec(memory_space=VMEM)
    smem = pl.BlockSpec(memory_space=pltpu.SMEM)
    anywhere = pl.BlockSpec(memory_space=pl.ANY)
    dma = pltpu.SemaphoreType.DMA

    def on_device(q, kv, go, act, down, upq, upkv, lengths, order):
        rows, width = q.shape[1], q.shape[2]
        head = kv.shape[3]
        group = width // head
        lanes = group * rows
        seq = rows * contexts
        slots = order.shape[0]
        docs = lengths.shape[1]
        rank = upq.shape[0]
        far = ys // 2
        kv = kv.reshape(2, rows, head)
        q, go, act = q.reshape(rows, width), go.reshape(rows, width), act.reshape(rows, width)
        wide = width // ys
        norm = ADAPTER_SCALE / math.sqrt(xs * seq)

        grad_q, grad_kv, sum_a, sum_b = pl.pallas_call(
            functools.partial(fused_kernel, ys, xs, heads, group, slots, docs, norm),
            out_shape=(
                jax.ShapeDtypeStruct((rows, width), BF16),
                jax.ShapeDtypeStruct((2, rows, head), BF16),
                jax.ShapeDtypeStruct((ys, 3 * rank, wide), BF16),
                jax.ShapeDtypeStruct((ys, 2 * rank, wide), BF16),
            ),
            in_specs=[smem, smem] + [anywhere] * 4 + [vmem] * 3,
            out_specs=(anywhere, vmem, vmem, vmem),
            scratch_shapes=[
                VMEM((2, contexts, rows, head), BF16),
                VMEM((lanes, head), BF16),
                VMEM((lanes, head), BF16),
                VMEM((rows, width), BF16),
                VMEM((contexts, rows, lanes), F32),
                VMEM((contexts, rows, lanes), F32),
                VMEM((3, 8, lanes), F32),
                VMEM((2, 8, lanes), jnp.int32),
                VMEM((head, lanes), F32),
                VMEM((2, 2, rows, head), F32),
                VMEM((rows, width), BF16),
                VMEM((2, 2, 2, far, rows, head), BF16),
                VMEM((2, 2, 2, far, rows, head), BF16),
                VMEM((2, 2, rows, head), BF16),
                VMEM((2, 3 * rank, rows), BF16),
                VMEM((chips, 3 * rank, rows), BF16),
                VMEM((3 * rank, rows), BF16),
                VMEM((2 * rank, rows), BF16),
                VMEM((2, rank, rows), BF16),
                VMEM((chips, rank, rows), BF16),
                VMEM((2, 2, 2 * rank, rows), BF16),
                VMEM((2 * rank, rows), BF16),
                VMEM((2 * chips, 2 * rank, rows), BF16),
                VMEM((ys, 3 * rank, wide), BF16),
                VMEM((ys, 3 * rank, wide), BF16),
                VMEM((ys, 2 * rank, wide), BF16),
                VMEM((ys, 2 * rank, wide), BF16),
                VMEM((team, 3 * rank, wide), BF16),
                VMEM((team, 2 * rank, wide), BF16),
                dma((3, group)),
                dma,
                dma((2,)),
                dma((2, 2, far, 2)),
                dma((2, 2, far, 2)),
                dma((2, 2, 2, far)),
                dma((2, 2, 2, far)),
                dma((2,)),
                dma((2,)),
                dma((1,)),
                dma((1,)),
                dma((chips - 1,)),
                dma((chips - 1,)),
                dma((2,)),
                dma((1,)),
                dma((1,)),
                dma((chips - 1,)),
                dma((chips - 1,)),
                dma((1,)),
                dma((1,)),
                dma((chips - 1,)),
                dma((chips - 1,)),
                dma((chips,)),
                dma((chips,)),
            ]
            + [dma((ys - 1,))] * 4
            + [dma((team - 1,))] * 4
            + [dma((ys - 1,))] * 4,
            compiler_params=pltpu.CompilerParams(
                collective_id=0, has_side_effects=True, vmem_limit_bytes=56 << 20
            ),
            name="attention_and_adapter_grads",
        )(order, lengths, q, kv, go, act, down.reshape(3 * rank, width), upq, upkv)

        gq, gkv, gdown, gupq, gupkv = pl.pallas_call(
            functools.partial(unpack_kernel, ys, rank),
            out_shape=(
                jax.ShapeDtypeStruct((rows, width), BF16),
                jax.ShapeDtypeStruct((2, rows, head), BF16),
                jax.ShapeDtypeStruct((3 * rank, width), F32),
                jax.ShapeDtypeStruct((rank, width), F32),
                jax.ShapeDtypeStruct((2, rank, head), F32),
            ),
            in_specs=[vmem] * 4,
            out_specs=(vmem,) * 5,
            name="write_outputs",
        )(sum_a, sum_b, grad_q, grad_kv)
        return (
            gq.reshape(1, rows, width),
            gkv.reshape(2, 1, rows, head),
            gdown.reshape(3, rank, width),
            gupq,
            gupkv,
        )

    return jax.shard_map(
        on_device,
        mesh=mesh,
        in_specs=(
            P("dp", "ctx", "head"),
            P(None, "dp", "ctx", "head"),
            P("dp", "ctx", "head"),
            P("dp", "ctx", "head"),
            P(None, None, "head"),
            P(None, "head"),
            P(None, None, "head"),
            P("dp", None),
            P(),
        ),
        out_specs=(
            P("dp", "ctx", "head"),
            P(None, "dp", "ctx", "head"),
            P(None, None, "head"),
            P(None, "head"),
            P(None, None, "head"),
        ),
        check_vma=False,
    )
```

```python
import functools
import math

import jax
import jax.numpy as jnp
from jax import lax
from jax.experimental import pallas as pl
from jax.experimental.pallas import tpu as pltpu
from jax.sharding import PartitionSpec as P

MESH = pl.DeviceIdType.MESH
BF16 = jnp.bfloat16
F32 = jnp.float32
VMEM = pltpu.VMEM
NT = (((1,), (1,)), ((), ()))
NN = (((1,), (0,)), ((), ()))
TN = (((0,), (0,)), ((), ()))
ADAPTER_SCALE = 2.0
NEG_LARGE = -1e30
BLOCK_LANES = 256
GATHER_LAG = 2


def dot(a, b, dims):
    return lax.dot_general(a, b, dims, preferred_element_type=F32)


def remote(src, dst, send_sem, recv_sem, device):
    return pltpu.make_async_remote_copy(
        src_ref=src,
        dst_ref=dst,
        send_sem=send_sem,
        recv_sem=recv_sem,
        device_id=device,
        device_id_type=MESH,
    )


def greet(devices):
    barrier = pltpu.get_barrier_semaphore()
    for device in devices:
        pl.semaphore_signal(barrier, inc=1, device_id=device, device_id_type=MESH)
    return barrier


def farthest(size):
    return sorted(range(size - 1), key=lambda k: -min(k + 1, size - 1 - k))


def fused_kernel(
    ys, xs, heads, group, slots_n, docs, norm,
    order_ref, lengths_ref, q_ref, kv_ref, go_ref, act_ref, down_ref, upq_ref, upkv_ref,
    gq_ref, gkv_ref, sum_a, sum_b,
    kv_all, q_st, g_st, act_v, s_scr, p_scr, stats, limits, gq_t, own, gq_v,
    ring_out, ring_in, cross, low_a, low_a2, low_mine, low_other, low_q, low_q2,
    low_kv, low_kv_out, low_kv2, ya_out, ya_in, yb_out, yb_in, ga_in, gb_in,
    in_sems, out_sem, z_sems, gather_send, gather_recv, ring_send, ring_recv, cross_send, cross_recv,
    la_send, la_recv, la2_send, la2_recv, lo_sems, lq_send, lq_recv, lq2_send, lq2_recv,
    lk_send, lk_recv, lk2_send, lk2_recv, lz_send, lz_recv,
    ya_send, ya_recv, yb_send, yb_recv, ga_send, ga_recv, gb_send, gb_recv,
    aa_send, aa_recv, ab_send, ab_recv,
):
    dp, c, h = lax.axis_index("dp"), lax.axis_index("ctx"), lax.axis_index("head")
    y, z = c % ys, c // ys
    far = ys // 2
    contexts = 2 * ys
    rows, head = kv_ref.shape[1], kv_ref.shape[2]
    rank = upq_ref.shape[0]
    block = rows // 2
    lanes = group * rows
    team = 2 * xs
    factor = 1.0 / math.sqrt(head)
    pieces = lanes // BLOCK_LANES
    tall = rows // 8

    across = (1 - z) * ys + y
    partner = {"ctx": across}
    right = {"ctx": z * ys + (y + 1) % ys}
    left = {"ctx": z * ys + (y + ys - 1) % ys}
    y_peers = [{"ctx": z * ys + (y + k) % ys} for k in range(1, ys)]
    chips = heads // 2
    core, chip = h % 2, h // 2
    pair_peers = [{"head": chip * 2 + 1 - core}]
    chip_heads = [(chip + k) % chips * 2 + core for k in range(chips)]
    chip_peers = [{"head": other} for other in chip_heads[1:]]
    z_peers = [{"ctx": across, "head": other} for other in chip_heads]
    me_t = dp * 2 + z
    t_peers = []
    for k in range(1, team):
        other = (me_t + k) % team
        t_peers.append({"dp": other // 2, "ctx": (other % 2) * ys + y})
    everyone = t_peers + z_peers[1:] + y_peers + chip_peers + pair_peers
    barrier = greet(everyone)
    kv_copy = pltpu.make_async_copy(kv_ref, kv_all.at[:, c], in_sems.at[2, 0])
    act_copy = pltpu.make_async_copy(act_ref, act_v, in_sems.at[2, 1])
    kv_copy.start()
    act_copy.start()
    copies = []
    for g in range(group):
        to = pl.ds(g * rows, rows)
        of = pl.ds(g * head, head)
        copies.append(pltpu.make_async_copy(q_ref.at[:, of], q_st.at[to], in_sems.at[0, g]))
        copies.append(pltpu.make_async_copy(go_ref.at[:, of], g_st.at[to], in_sems.at[1, g]))
    for copy in copies:
        copy.start()

    kv_copy.wait()
    pl.semaphore_wait(barrier, len(everyone))

    def spread(buffer, me, peers, size, send, recv):
        def one(k, slot):
            return remote(
                buffer.at[slot], buffer.at[slot], send.at[k], recv.at[k], peers[k]
            )

        def start():
            for k in farthest(size):
                one(k, me).start()

        def arrive():
            for k in range(size - 1):
                one(k, (me + size - 1 - k) % size).wait_recv()

        def drain():
            for k in range(size - 1):
                one(k, me).wait_send()

        return start, arrive, drain

    def exchange(out, held, send, recv):
        def one(k, to, slot):
            return remote(out.at[to], held.at[slot], send.at[k], recv.at[k], y_peers[k])

        def start():
            for k in farthest(ys):
                one(k, (y + 1 + k) % ys, y).start()
            held[y] = out[y]

        def arrive():
            for k in range(ys - 1):
                one(k, 0, (y + ys - 1 - k) % ys).wait_recv()

        def drain():
            for k in range(ys - 1):
                one(k, (y + 1 + k) % ys, y).wait_send()

        return start, arrive, drain

    def total_of(buffer, size):
        total = buffer[0].astype(F32)
        for k in range(1, size):
            total = total + buffer[k].astype(F32)
        return total

    cross_kv = remote(
        kv_all.at[:, c], kv_all.at[:, c], z_sems.at[0], z_sems.at[1], partner
    )
    cross_kv.start()

    def line(u):
        return (z + u * (1 - 2 * z)) * ys

    def hop(u, d, a, j, here):
        slot = line(u) + (y + 2 * ys + (2 * d - 1) * here) % ys
        whole = False
        ref = kv_all.at[:, slot] if whole else kv_all.at[j, slot]
        away = 2 if u == 1 and a == far else 1
        to = (y + away) % ys if d == 0 else (y + ys - away) % ys
        return remote(
            ref, ref, gather_send.at[u, d, a - 1, j], gather_recv.at[u, d, a - 1, j],
            {"ctx": z * ys + to},
        )

    def sent(u, d, a, j):
        return hop(u, d, a, j, a - 2 if u == 1 and a == far else a - 1)

    def landed(u, d, a, j):
        return hop(u, d, a, j, a)

    def messages(u, a):
        if a == far:
            return [(d, d) for d in range(2)]
        return [(d, j) for j in range(2) for d in range(2)]

    for d, j in messages(0, 1):
        sent(0, d, 1, j).start()
    la_start, la_arrive, la_drain = spread(low_a, core, pair_peers, 2, la_send, la_recv)
    la2_start, la2_arrive, la2_drain = spread(
        low_a2, chip, chip_peers, chips, la2_send, la2_recv
    )
    act_copy.wait()
    act = act_v[...]
    low_a[core] = dot(down_ref[...], act, NT).astype(BF16)
    la_start()
    lane = lax.broadcasted_iota(jnp.int32, (8, lanes), 1)
    row = lane
    for g in range(1, group):
        row = jnp.where(lane >= g * rows, lane - g * rows, row)
    first = order_ref[2 * c] * block
    second = order_ref[2 * c + 1] * block - block
    pos = row + jnp.where(row < block, first, second)
    begin = jnp.zeros((8, lanes), jnp.int32)
    bound = 0
    for i in range(docs):
        bound = bound + lengths_ref[0, i]
        begin = jnp.where(pos >= bound, bound, begin)
    limits[0] = begin
    limits[1] = pos
    stats[0] = jnp.full((8, lanes), NEG_LARGE, F32)
    stats[1] = jnp.zeros((8, lanes), F32)
    stats[2] = jnp.zeros((8, lanes), F32)
    gq_t[...] = jnp.zeros(gq_t.shape, F32)
    for copy in copies:
        copy.wait()
    sub = lax.broadcasted_iota(jnp.int32, (rows, BLOCK_LANES), 0)
    sub = sub.reshape(tall, 8, BLOCK_LANES)

    def score(slot):
        keys, values = kv_all[0, slot], kv_all[1, slot]
        upper = order_ref[2 * slot] * block
        lower = order_ref[2 * slot + 1] * block - block
        place = sub + jnp.where(sub < block, upper, lower)
        for i in range(pieces):
            at = slice(i * BLOCK_LANES, (i + 1) * BLOCK_LANES)
            s = dot(keys, q_st[at], NT) * (factor * math.log2(math.e))
            s = s.reshape(tall, 8, BLOCK_LANES)
            seen = (place >= limits[0, :, at]) & (place <= limits[1, :, at])
            s = jnp.where(seen, s, NEG_LARGE)
            s_scr[slot, :, at] = s.reshape(rows, BLOCK_LANES)
            d = dot(values, g_st[at], NT)
            p_scr[slot, :, at] = d
            before = stats[0, :, at]
            most = jnp.maximum(before, jnp.max(s, axis=0))
            w = jnp.exp2(s - most)
            shrink = jnp.exp2(before - most)
            stats[0, :, at] = most
            stats[1, :, at] = stats[1, :, at] * shrink + jnp.sum(w, axis=0)
            stats[2, :, at] = stats[2, :, at] * shrink + jnp.sum(
                w * d.reshape(tall, 8, BLOCK_LANES), axis=0
            )

    lag = GATHER_LAG

    def gather_step(k, carry):
        u = k % 2
        n = k // 2 - lag * u
        s = (n + 1) // 2
        d = (n + 1) % 2

        for a in range(1, far + 1):

            @pl.when(k == 2 * (2 * a - 1))
            def _():
                for e, j in messages(0, a):
                    landed(0, e, a, j).wait_recv()
                    if a + 1 < far or (a + 1 == far and e == j):
                        sent(0, e, a + 1, j).start()

        @pl.when(k == 5)
        def _():
            cross_kv.wait_recv()
            for e, j in messages(1, 1):
                sent(1, e, 1, j).start()

        @pl.when(k == 7)
        def _():
            la_arrive()
            low_a2[chip] = total_of(low_a, 2).astype(BF16)
            la2_start()

        for a, at in ((1, 1), (2, 3), (3, 5), (4, 7)):

            @pl.when(k == 2 * (at + lag) + 1)
            def _():
                for e, j in messages(1, a):
                    landed(1, e, a, j).wait_recv()
                    if a == far - 2 and e == j:
                        sent(1, e, far, j).start()
                    if a + 1 < far:
                        sent(1, e, a + 1, j).start()

        @pl.when((n >= 0) & (n < ys))
        def _():
            swap = 0
            score(line(u) + (y + 2 * ys + (2 * d - 1) * (s + swap)) % ys)

        return carry

    lax.fori_loop(0, 2 * ys + 2 * lag, gather_step, 0)

    most = jnp.max(stats[0], axis=0, keepdims=True)
    shrink = jnp.exp2(stats[0] - most)
    total = jnp.sum(stats[1] * shrink, axis=0, keepdims=True)
    slope = jnp.sum(stats[2] * shrink, axis=0, keepdims=True)
    stats[0] = jnp.broadcast_to(most + jnp.log2(total), (8, lanes))
    stats[1] = jnp.broadcast_to(slope / total, (8, lanes))

    def ring(j, d, u, away, to):
        return remote(
            ring_out.at[j, d, u, away - 1], ring_in.at[j, d, u, away - 1],
            ring_send.at[j, d, u, away - 1], ring_recv.at[j, d, u, away - 1], to,
        )

    low_x = remote(
        low_mine.at[pl.ds(rank, 2 * rank)], low_other, lo_sems.at[0], lo_sems.at[1], partner
    )

    skip = [{"ctx": z * ys + (y + 2) % ys}, {"ctx": z * ys + (y + ys - 2) % ys}]

    def reduce_step(k, carry):
        u = k % 2
        n = k // 2
        away = far - (n + 1) // 2
        d = (n + 1) % 2
        slot = line(1 - u) + (y + 2 * ys + (1 - 2 * d) * away) % ys
        keys = kv_all[0, slot]
        grad_k = jnp.zeros((rows, head), F32)
        grad_v = jnp.zeros((rows, head), F32)
        for i in range(pieces):
            at = slice(i * BLOCK_LANES, (i + 1) * BLOCK_LANES)
            s = s_scr[slot, :, at].reshape(tall, 8, BLOCK_LANES)
            prob = jnp.exp2(s - stats[0, :, at])
            tilt = p_scr[slot, :, at].reshape(tall, 8, BLOCK_LANES) - stats[1, :, at]
            ds = (prob * tilt).reshape(rows, BLOCK_LANES).astype(BF16)
            prob = prob.reshape(rows, BLOCK_LANES).astype(BF16)
            grad_v = grad_v + dot(prob, g_st[at], NN)
            grad_k = grad_k + dot(ds, q_st[at], NN)
            gq_t[:, at] += dot(keys, ds, TN)
        grads = (grad_k * factor, grad_v)

        @pl.when(k == 3)
        def _():
            la2_arrive()
            low_mine[...] = total_of(low_a2, chips).astype(BF16)
            low_x.start()

        @pl.when(n == 0)
        def _():
            for j in range(2):
                ring_out[j, j, u, far - 1] = grads[j].astype(BF16)
                ring(j, j, u, far, skip[j]).start()

        for e in range(2):
            to = right if e == 0 else left
            for a in range(far - 1, 0, -1):

                @pl.when((n > 0) & (n < ys - 1) & (d == e) & (away == a))
                def _():
                    for j in (1 - e, e):
                        part = grads[j]
                        if a < far - 1:
                            ring(j, e, u, a + 1, to).wait_recv()
                            part = part + ring_in[j, e, u, a].astype(F32)
                        if a == far - 2 and j == e:
                            ring(j, e, u, far, to).wait_recv()
                            part = part + ring_in[j, e, u, far - 1].astype(F32)
                        ring_out[j, e, u, a - 1] = part.astype(BF16)
                        ring(j, e, u, a, to).start()

        @pl.when(n == ys - 1)
        def _():
            for j in range(2):
                own[u, j] = grads[j]

        return carry

    lax.fori_loop(0, 2 * ys, reduce_step, 0)

    lq_start, lq_arrive, lq_drain = spread(low_q, core, pair_peers, 2, lq_send, lq_recv)
    lq2_start, lq2_arrive, lq2_drain = spread(
        low_q2, chip, chip_peers, chips, lq2_send, lq2_recv
    )
    lk_start, lk_arrive, lk_drain = spread(low_kv, core, pair_peers, 2, lk_send, lk_recv)
    gq = (gq_t[...] * factor).T.astype(BF16)
    for g in range(group):
        gq_v[:, g * head : (g + 1) * head] = gq[g * rows : (g + 1) * rows]
    gq_copy = pltpu.make_async_copy(gq_v, gq_ref, out_sem)
    gq_copy.start()
    gq = gq_v[...]
    low_q[core] = dot(upq_ref[...], gq, NT).astype(BF16)
    lq_start()
    low = low_mine[...]
    width = act.shape[1] // ys

    def cut(buffer, at, value):
        value = value.astype(BF16)
        for k in range(ys):
            buffer[k, at : at + value.shape[0], :] = value[:, k * width : (k + 1) * width]

    cut(ya_out, rank, dot(low[:rank], gq, NN))

    lq_arrive()
    low_q2[chip] = total_of(low_q, 2).astype(BF16)
    lq2_start()

    ends = []
    for u in range(2):
        pair = []
        for j in range(2):
            total = own[u, j]
            for d in range(2):
                ring(j, d, u, 1, right if d == 0 else left).wait_recv()
                total = total + ring_in[j, d, u, 0].astype(F32)
            pair.append(total)
        ends.append(pair)
    cross_hops = [
        remote(cross.at[0, j], cross.at[1, j], cross_send.at[j], cross_recv.at[j], partner)
        for j in range(2)
    ]
    theirs = [ends[0][j].astype(BF16) for j in range(2)]
    ours = [ends[1][j].astype(BF16) for j in range(2)]
    for j in range(2):
        at = slice(j * rank, (j + 1) * rank)
        low_kv[core, 0, at, :] = dot(upkv_ref[j], ours[j], NT).astype(BF16)
        low_kv[core, 1, at, :] = dot(upkv_ref[j], theirs[j], NT).astype(BF16)
    lk_start()
    me_k = z * chips + chip

    def same_hop(k, slot):
        return remote(
            low_kv2.at[slot], low_kv2.at[slot], lk2_send.at[k], lk2_recv.at[k], chip_peers[k]
        )

    def other_hop(k, slot):
        return remote(low_kv_out, low_kv2.at[slot], lz_send.at[k], lz_recv.at[k], z_peers[k])

    for j in range(2):
        cross[0, j] = theirs[j]
        own[1, j] = ends[1][j]
    low_x.wait_recv()
    ya_out[2:, 2 * rank :, :] = jnp.zeros((ys - 2, rank, width), BF16)
    for j in range(2):
        at = slice(j * rank, (j + 1) * rank)
        up = dot(low_mine[(1 + j) * rank : (2 + j) * rank], ours[j], NN)
        up = up + dot(low_other[at], theirs[j], NN)
        ya_out[j, 2 * rank :, :] = up.astype(BF16)
    lk_arrive()
    low_kv2[me_k] = (low_kv[0, 0].astype(F32) + low_kv[1, 0].astype(F32)).astype(BF16)
    low_kv_out[...] = (low_kv[0, 1].astype(F32) + low_kv[1, 1].astype(F32)).astype(BF16)
    for k in range(chips):
        other_hop(k, me_k).start()
    for k in range(chips - 1):
        same_hop(k, me_k).start()

    ya_start, ya_arrive, ya_drain = exchange(ya_out, ya_in, ya_send, ya_recv)
    yb_start, yb_arrive, yb_drain = exchange(yb_out, yb_in, yb_send, yb_recv)
    ga_start, ga_arrive, ga_drain = spread(ga_in, me_t, t_peers, team, ga_send, ga_recv)
    gb_start, gb_arrive, gb_drain = spread(gb_in, me_t, t_peers, team, gb_send, gb_recv)
    aa_start, aa_arrive, aa_drain = spread(sum_a, y, y_peers, ys, aa_send, aa_recv)
    ab_start, ab_arrive, ab_drain = spread(sum_b, y, y_peers, ys, ab_send, ab_recv)

    lq2_arrive()
    cut(ya_out, 0, dot(total_of(low_q2, chips).astype(BF16), act, NN))
    ya_start()
    for k in range(chips):
        other_hop(k, (1 - z) * chips + (chip + chips - k) % chips).wait_recv()
    for k in range(chips - 1):
        same_hop(k, z * chips + (chip + chips - 1 - k) % chips).wait_recv()
    cut(yb_out, 0, dot(total_of(low_kv2, 2 * chips).astype(BF16), act, NN))
    yb_start()
    ya_arrive()
    ga_in[me_t] = total_of(ya_in, ys).astype(BF16)
    ga_start()
    yb_arrive()
    gb_in[me_t] = total_of(yb_in, ys).astype(BF16)
    gb_start()
    ga_arrive()
    sum_a[y] = (total_of(ga_in, team) * norm).astype(BF16)
    aa_start()
    gb_arrive()
    for j in range(2):
        cross_hops[j].start()
    sum_b[y] = (total_of(gb_in, team) * norm).astype(BF16)
    ab_start()
    for j in range(2):
        cross_hops[j].wait_recv()
        gkv_ref[j] = (own[1, j] + cross[1, j].astype(F32)).astype(BF16)
    la_drain()
    la2_drain()
    lq_drain()
    lq2_drain()
    lk_drain()
    ya_drain()
    yb_drain()
    ga_drain()
    gb_drain()
    low_x.wait_send()
    cross_kv.wait_send()
    for k in range(chips):
        other_hop(k, me_k).wait_send()
    for k in range(chips - 1):
        same_hop(k, me_k).wait_send()
    for u in range(2):
        for a in range(1, far + 1):
            for d, j in messages(u, a):
                sent(u, d, a, j).wait_send()
    for j in range(2):
        cross_hops[j].wait_send()
        for d in range(2):
            for u in range(2):
                for away in range(1, far + (j == d)):
                    ring(j, d, u, away, right if d == 0 else left).wait_send()
    aa_arrive()
    ab_arrive()
    aa_drain()
    ab_drain()
    gq_copy.wait()


def unpack_kernel(
    ys, rank, sum_a, sum_b, gq_in, gkv_in, gq_ref, gkv_ref, gdown_ref, gupq_ref, gupkv_ref
):
    gq_ref[...] = gq_in[...]
    gkv_ref[...] = gkv_in[...]
    width = sum_a.shape[2]
    for k in range(ys):
        at = slice(k * width, (k + 1) * width)
        gdown_ref[:rank, at] = sum_a[k, :rank].astype(F32)
        gupq_ref[:, at] = sum_a[k, rank : 2 * rank].astype(F32)
        gdown_ref[rank:, at] = sum_b[k].astype(F32)
    for j in range(2):
        gupkv_ref[j] = sum_a[j, 2 * rank :].astype(F32)


def solution(mesh):
    contexts, heads, xs = mesh.shape["ctx"], mesh.shape["head"], mesh.shape["dp"]
    ys = contexts // 2
    team, chips = 2 * xs, heads // 2
    vmem = pl.BlockSpec(memory_space=VMEM)
    smem = pl.BlockSpec(memory_space=pltpu.SMEM)
    anywhere = pl.BlockSpec(memory_space=pl.ANY)
    dma = pltpu.SemaphoreType.DMA

    def on_device(q, kv, go, act, down, upq, upkv, lengths, order):
        rows, width = q.shape[1], q.shape[2]
        head = kv.shape[3]
        group = width // head
        lanes = group * rows
        seq = rows * contexts
        slots = order.shape[0]
        docs = lengths.shape[1]
        rank = upq.shape[0]
        far = ys // 2
        kv = kv.reshape(2, rows, head)
        q, go, act = q.reshape(rows, width), go.reshape(rows, width), act.reshape(rows, width)
        wide = width // ys
        norm = ADAPTER_SCALE / math.sqrt(xs * seq)

        grad_q, grad_kv, sum_a, sum_b = pl.pallas_call(
            functools.partial(fused_kernel, ys, xs, heads, group, slots, docs, norm),
            out_shape=(
                jax.ShapeDtypeStruct((rows, width), BF16),
                jax.ShapeDtypeStruct((2, rows, head), BF16),
                jax.ShapeDtypeStruct((ys, 3 * rank, wide), BF16),
                jax.ShapeDtypeStruct((ys, 2 * rank, wide), BF16),
            ),
            in_specs=[smem, smem] + [anywhere] * 4 + [vmem] * 3,
            out_specs=(anywhere, vmem, vmem, vmem),
            scratch_shapes=[
                VMEM((2, contexts, rows, head), BF16),
                VMEM((lanes, head), BF16),
                VMEM((lanes, head), BF16),
                VMEM((rows, width), BF16),
                VMEM((contexts, rows, lanes), F32),
                VMEM((contexts, rows, lanes), F32),
                VMEM((3, 8, lanes), F32),
                VMEM((2, 8, lanes), jnp.int32),
                VMEM((head, lanes), F32),
                VMEM((2, 2, rows, head), F32),
                VMEM((rows, width), BF16),
                VMEM((2, 2, 2, far, rows, head), BF16),
                VMEM((2, 2, 2, far, rows, head), BF16),
                VMEM((2, 2, rows, head), BF16),
                VMEM((2, 3 * rank, rows), BF16),
                VMEM((chips, 3 * rank, rows), BF16),
                VMEM((3 * rank, rows), BF16),
                VMEM((2 * rank, rows), BF16),
                VMEM((2, rank, rows), BF16),
                VMEM((chips, rank, rows), BF16),
                VMEM((2, 2, 2 * rank, rows), BF16),
                VMEM((2 * rank, rows), BF16),
                VMEM((2 * chips, 2 * rank, rows), BF16),
                VMEM((ys, 3 * rank, wide), BF16),
                VMEM((ys, 3 * rank, wide), BF16),
                VMEM((ys, 2 * rank, wide), BF16),
                VMEM((ys, 2 * rank, wide), BF16),
                VMEM((team, 3 * rank, wide), BF16),
                VMEM((team, 2 * rank, wide), BF16),
                dma((3, group)),
                dma,
                dma((2,)),
                dma((2, 2, far, 2)),
                dma((2, 2, far, 2)),
                dma((2, 2, 2, far)),
                dma((2, 2, 2, far)),
                dma((2,)),
                dma((2,)),
                dma((1,)),
                dma((1,)),
                dma((chips - 1,)),
                dma((chips - 1,)),
                dma((2,)),
                dma((1,)),
                dma((1,)),
                dma((chips - 1,)),
                dma((chips - 1,)),
                dma((1,)),
                dma((1,)),
                dma((chips - 1,)),
                dma((chips - 1,)),
                dma((chips,)),
                dma((chips,)),
            ]
            + [dma((ys - 1,))] * 4
            + [dma((team - 1,))] * 4
            + [dma((ys - 1,))] * 4,
            compiler_params=pltpu.CompilerParams(
                collective_id=0, has_side_effects=True, vmem_limit_bytes=56 << 20
            ),
            name="attention_and_adapter_grads",
        )(order, lengths, q, kv, go, act, down.reshape(3 * rank, width), upq, upkv)

        gq, gkv, gdown, gupq, gupkv = pl.pallas_call(
            functools.partial(unpack_kernel, ys, rank),
            out_shape=(
                jax.ShapeDtypeStruct((rows, width), BF16),
                jax.ShapeDtypeStruct((2, rows, head), BF16),
                jax.ShapeDtypeStruct((3 * rank, width), F32),
                jax.ShapeDtypeStruct((rank, width), F32),
                jax.ShapeDtypeStruct((2, rank, head), F32),
            ),
            in_specs=[vmem] * 4,
            out_specs=(vmem,) * 5,
            name="write_outputs",
        )(sum_a, sum_b, grad_q, grad_kv)
        return (
            gq.reshape(1, rows, width),
            gkv.reshape(2, 1, rows, head),
            gdown.reshape(3, rank, width),
            gupq,
            gupkv,
        )

    return jax.shard_map(
        on_device,
        mesh=mesh,
        in_specs=(
            P("dp", "ctx", "head"),
            P(None, "dp", "ctx", "head"),
            P("dp", "ctx", "head"),
            P("dp", "ctx", "head"),
            P(None, None, "head"),
            P(None, "head"),
            P(None, None, "head"),
            P("dp", None),
            P(),
        ),
        out_specs=(
            P("dp", "ctx", "head"),
            P(None, "dp", "ctx", "head"),
            P(None, None, "head"),
            P(None, "head"),
            P(None, None, "head"),
        ),
        check_vma=False,
    )
```
